32 devices in a mesh: grp: 2 (over y), blk: 16 (over z, x, core).
Axes of the slice: x: 2, y: 2, z: 4, core: 2. Of those that a mesh axis runs over, the one named last changes fastest.
Arguments:
- tokens: bfloat16 [4096, 2048], P(('grp', 'blk')), may hold values from -6 to 6
- d_out: bfloat16 [4096, 2048], P(('grp', 'blk')), may hold values from -6 to 6
- expert_ids: int32 [4096, 6], P(('grp', 'blk')), may hold values from 0 to 15, all different within a row; in each aligned block of 128 rows (0 to 127, 128 to 255, ...) at most 52 rows name the same one
- gate_values: bfloat16 [4096, 6], P(('grp', 'blk')), may hold values from 0.049804688 to 0.44921875
- saved_gate_pre: bfloat16 [4096, 6, 704], P(('grp', 'blk')), may hold values from -6 to 6
- saved_up_pre: bfloat16 [4096, 6, 704], P(('grp', 'blk')), may hold values from -6 to 6
- w_gate: bfloat16 [16, 2048, 704], P('blk'), may hold values from -0.125 to 0.125
- w_up: bfloat16 [16, 2048, 704], P('blk'), may hold values from -0.125 to 0.125
- w_down: bfloat16 [16, 704, 2048], P('blk'), may hold values from -0.21875 to 0.21875
Outputs:
- d_tokens: bfloat16 [4096, 2048], P(('grp', 'blk'))
- d_w_gate: bfloat16 [16, 2048, 704], P('blk', 'grp')
- d_w_up: bfloat16 [16, 2048, 704], P('blk', 'grp')
- d_w_down: bfloat16 [16, 704, 2048], P('blk', None, 'grp')
The draws below stay inside these ranges and needn't reach their ends.
Inputs may be any that keep to these rules, and one draw needn't show every extreme that they name: `expert_ids`: within the 128 rows of one device no expert is named more than 52 times, a bound that some block reaches; the 6 ids of a token differ.
All inputs are finite; a program needn't handle non-finite values.
Results may differ from the reference program's by a relative error of at most 0.0057.
Values may be sent and summed in bfloat16 or wider, within the bound.
No kernel may reach another device: no remote copies, remote signals or barrier semaphores. Data moves between devices by JAX's collectives and lax.ppermute only.
A program may use at most 192 MiB of HBM per device.

```python
import math
import jax
import jax.numpy as jnp
import numpy as np
from jax import lax

D = 2048
TOPK = 6
FFW = 704
TOK_DEV = 128
EXPERTS = 16
CAP = 52
TOKENS = 4096
N_GRP = 2
N_BLK = 16


def with_spikes(entries, own_key, source, target, shards_of, factor):
    owner, partner = [(jnp.arange(entries.shape[position]) // (entries.shape[position] // shards_of)).reshape([-1 if axis == position else 1 for axis in range(entries.ndim)]) for position in (source, target)]
    chosen = jax.random.permutation(own_key, shards_of)[partner]
    strong = (owner == chosen) | (owner == (partner + shards_of // 2) % shards_of)
    return jnp.where(strong, factor * entries, entries)


def block_scale(stream_key, extent, shards, least, largest):
    factor_of, own = 1.0, jax.random.fold_in(stream_key, 6)
    for axis_at, parts in shards:
        draws = jnp.exp(jax.random.uniform(jax.random.fold_in(own, axis_at), (parts,), jnp.float32, least / len(shards), largest / len(shards)))
        factor_of = factor_of * jnp.repeat(draws, extent[axis_at] // parts).reshape([-1 if axis == axis_at else 1 for axis in range(len(extent))])
    return factor_of


def routed_block(own_key, own, number, rows, amount, top, most, lean):
    order = jax.random.permutation(own_key, amount)
    packed, ordinary = load_shares(amount, rows * top, most, lean, True), load_shares(amount, rows * top, most, lean, False)
    places = jnp.arange(amount)

    def named(sizes, turn):
        used = int((sizes > 0).sum())
        fixed = max(1, used // 4)
        moved = fixed + (places - fixed + turn * (used - fixed)) % max(1, amount - fixed)
        return jnp.zeros((amount,), jnp.int32).at[order[jnp.where(places < fixed, places, moved)]].set(jnp.asarray(sizes, jnp.int32))

    sizes = jnp.where(number % 4 == 0, named(packed, number // 4), named(ordinary, number - number // 4 - 1))
    mixed = jax.random.permutation(jax.random.fold_in(own, 3), amount)
    giver, sink = mixed[0:amount // 2 * 2:2], mixed[1:amount // 2 * 2:2]
    room = jnp.minimum(sizes[giver] - 1, most - sizes[sink]) // 2
    room = jnp.where((giver == order[0]) | (sink == order[0]) | (sizes[sink] == 0), 0, jnp.maximum(room, 0))
    moved = jax.random.randint(jax.random.fold_in(own, 4), (amount // 2,), 0, 1 << 20) % (room + 1)
    sizes = sizes.at[giver].add(-moved).at[sink].add(moved)
    members = jnp.searchsorted(jnp.cumsum(sizes), jnp.arange(rows * top), side="right").astype(jnp.int32)
    grid = members.reshape(top, rows).T
    grid = grid[jax.random.permutation(jax.random.fold_in(own, 1), rows)]
    turn = jax.random.randint(jax.random.fold_in(own, 2), (rows, 1), 0, top)
    return jnp.take_along_axis(grid, (jnp.arange(top)[None, :] + turn) % top, axis=1)


def load_shares(amount, total, reach, slope, full):
    loads = [(1 << 20) // math.isqrt(grade ** slope) + 1 for grade in range(1, amount + 1)]
    largest = reach if full else min(reach, max(-(-total // amount), total * loads[0] // sum(loads)))
    least = 1 if total - largest >= amount - 1 else 0
    given, rest = [largest] + [least] * (amount - 1), total - largest - least * (amount - 1)
    while rest > 0:
        movable = [i for i in range(1, amount) if given[i] < largest] or [i for i in range(1, amount) if given[i] < reach]
        mass, remaining = sum([loads[i] for i in movable]), rest
        for i in movable:
            extra = min(reach - given[i], max(1, remaining * loads[i] // mass), rest)
            given[i] = given[i] + extra
            rest = rest - extra
    return np.array(given)


def normal_values(rng, dims, deviation, bound, pieces=(), held_as=jnp.bfloat16):
    result = jax.random.normal(rng, dims, jnp.float32) * deviation
    if len(pieces) > 0:
        result = block_scale(rng, dims, pieces, -0.22, 0.18) * result
    return jnp.clip(result, min=-bound, max=bound).astype(held_as)


def gaussian_with(own_key, extent, deviation, reach, cuts, heavy, held_as=jnp.bfloat16):
    values = deviation * jax.random.normal(own_key, extent, jnp.float32)
    if cuts:
        values = values * block_scale(own_key, extent, cuts, -0.22, 0.18)
    return jnp.clip(with_spikes(values, jax.random.fold_in(own_key, 3), *heavy), -reach, reach).astype(held_as)


def setup_inputs(seed: int = 0) -> dict:
    key_of = jax.random.split(jax.random.key(seed), 10)
    tokens = normal_values(key_of[0], (TOKENS, D), 1.0, 6.0, ((0, 32),))
    d_out = gaussian_with(key_of[1], (TOKENS, D), 1.0, 6.0, ((0, 32),), (0, 1, 32, 2.75))
    expert_ids_keys = jax.random.split(jax.random.fold_in(key_of[2], 1), TOKENS // TOK_DEV)
    expert_ids_turns = jax.random.permutation(jax.random.fold_in(key_of[2], 3), TOKENS // TOK_DEV)
    expert_ids = jax.vmap(lambda own, number: routed_block(jax.random.fold_in(key_of[2], 2), own, number, TOK_DEV, EXPERTS, TOPK, CAP, 2))(expert_ids_keys, expert_ids_turns).reshape((TOKENS, TOPK))
    gate_values = jnp.clip(0.049804688 + 0.39941406 * jax.random.uniform(key_of[3], (TOKENS, TOPK), jnp.float32) ** block_scale(key_of[3], (TOKENS, TOPK), ((0, 32),), -0.2, 0.2), 0.049804688, 0.44921875).astype(jnp.bfloat16)
    saved_gate_pre = normal_values(key_of[4], (TOKENS, TOPK, FFW), 1.0, 6.0, ((0, 32),))
    saved_up_pre = normal_values(key_of[5], (TOKENS, TOPK, FFW), 1.0, 6.0, ((0, 32),))
    w_gate = normal_values(key_of[6], (EXPERTS, D, FFW), D ** -0.5, 0.125, ((0, 16),))
    w_up = normal_values(key_of[7], (EXPERTS, D, FFW), D ** -0.5, 0.125, ((0, 16),))
    w_down = normal_values(key_of[8], (EXPERTS, FFW, D), FFW ** -0.5, 0.21875, ((0, 16),))
    return {"tokens": tokens, "d_out": d_out, "expert_ids": expert_ids, "gate_values": gate_values, "saved_gate_pre": saved_gate_pre, "saved_up_pre": saved_up_pre, "w_gate": w_gate, "w_up": w_up, "w_down": w_down}


def expert_backward(inputs, cotangents, weights, gate_pre, up_pre, gate_mat, up_mat, down_mat):
    sigmoid_gate = jax.nn.sigmoid(gate_pre)
    active = gate_pre * sigmoid_gate
    scaled_hidden = (weights[:, None] * active * up_pre).astype(jnp.bfloat16)
    back_hidden = weights[:, None] * jnp.dot(cotangents, down_mat.T, preferred_element_type=jnp.float32)
    grad_gate = (back_hidden * up_pre * sigmoid_gate * (1.0 + gate_pre * (1.0 - sigmoid_gate))).astype(jnp.bfloat16)
    grad_up = (back_hidden * active).astype(jnp.bfloat16)
    route_grad = (jnp.dot(grad_gate, gate_mat.T, preferred_element_type=jnp.float32)
                  + jnp.dot(grad_up, up_mat.T, preferred_element_type=jnp.float32)).astype(jnp.bfloat16)
    sum_gate = jnp.dot(inputs.T, grad_gate, preferred_element_type=jnp.float32)
    sum_up = jnp.dot(inputs.T, grad_up, preferred_element_type=jnp.float32)
    sum_down = jnp.dot(scaled_hidden.T, cotangents, preferred_element_type=jnp.float32)
    return route_grad, sum_gate, sum_up, sum_down


def reference(tokens, d_out, expert_ids, gate_values, saved_gate_pre, saved_up_pre, w_gate, w_up, w_down):
    routes_total = TOKENS * TOPK
    most_rows = N_GRP * N_BLK * CAP
    flat_ids = expert_ids.reshape(-1)
    flat_gate = gate_values.reshape(-1).astype(jnp.float32)
    flat_gate_pre = saved_gate_pre.reshape(routes_total, FFW)
    flat_up_pre = saved_up_pre.reshape(routes_total, FFW)

    def one_expert(grad_accum, expert):
        positions = jnp.nonzero(flat_ids == expert, size=most_rows, fill_value=routes_total)[0].astype(jnp.int32)
        present = positions < routes_total
        clipped = jnp.minimum(positions, routes_total - 1)
        owner = clipped // TOPK
        weights = jnp.where(present, flat_gate[clipped], jnp.zeros_like(flat_gate[clipped]))
        inputs = jnp.where(present[:, None], tokens[owner], jnp.zeros_like(tokens[owner]))
        cotangents = jnp.where(present[:, None], d_out[owner], jnp.zeros_like(d_out[owner]))
        gate_pre = flat_gate_pre[clipped].astype(jnp.float32)
        up_pre = flat_up_pre[clipped].astype(jnp.float32)
        route_grad, sum_gate, sum_up, sum_down = expert_backward(
            inputs, cotangents, weights, gate_pre, up_pre, w_gate[expert], w_up[expert], w_down[expert])
        route_grad = jnp.where(present[:, None], route_grad.astype(jnp.float32), jnp.zeros((most_rows, D), jnp.float32))
        grad_accum = grad_accum.at[owner].add(route_grad)
        return grad_accum, (sum_gate.astype(jnp.bfloat16), sum_up.astype(jnp.bfloat16), sum_down.astype(jnp.bfloat16))

    start_accum = jnp.zeros((TOKENS, D), jnp.float32)
    grad_accum, stacked = lax.scan(one_expert, start_accum, jnp.arange(EXPERTS, dtype=jnp.int32))
    return grad_accum.astype(jnp.bfloat16), stacked[0], stacked[1], stacked[2]
```

```python
import functools

import jax
import jax.numpy as jnp
from jax import lax
from jax.experimental import pallas as pl
from jax.experimental.pallas import tpu as pltpu
from jax.sharding import PartitionSpec as P

BF16 = jnp.bfloat16
F32 = jnp.float32
VMEM_BYTES = 56 * 1024 * 1024
NT = (((1,), (1,)), ((), ()))
TN = (((0,), (0,)), ((), ()))


def params():
    return pltpu.CompilerParams(vmem_limit_bytes=VMEM_BYTES)


def cost(flops, moved):
    return pl.CostEstimate(flops=int(flops), bytes_accessed=int(moved), transcendentals=0)


def dot(a, b):
    return jnp.dot(a, b, preferred_element_type=F32)


def before_matrix(size):
    row = lax.broadcasted_iota(jnp.int32, (size, size), 0)
    col = lax.broadcasted_iota(jnp.int32, (size, size), 1)
    return jnp.where(row < col, 1.0, 0.0).astype(BF16)


def expert_hits(meta, top, expert):
    hits = jnp.where(meta[:top] == expert, 1.0, 0.0)
    return jnp.sum(hits, axis=0, keepdims=True), jnp.sum(hits * meta[top:], axis=0, keepdims=True)


def chip_slots(own, sib, core, before):
    rows = jnp.broadcast_to(own, (8, own.shape[1])), jnp.broadcast_to(sib, (8, sib.shape[1]))
    own_before = dot(rows[0].astype(BF16), before)[:1]
    sib_before = dot(rows[1].astype(BF16), before)[:1]
    own_total = jnp.sum(own, axis=1, keepdims=True)
    sib_total = jnp.sum(sib, axis=1, keepdims=True)
    core_f = core.astype(F32)
    own_slot = jnp.where(own > 0, own_before + core_f * sib_total, -1.0)
    sib_slot = jnp.where(sib > 0, sib_before + (1.0 - core_f) * own_total, -1.0)
    return own_slot, sib_slot


def slot_rows(slot, count):
    row = lax.broadcasted_iota(jnp.int32, (count, slot.shape[1]), 0).astype(F32)
    return jnp.where(row == slot, 1.0, 0.0)


def pack_kernel(zn, top, chip_rows, sc, meta_own, meta_sib, *refs):
    srcs, outs, (cat, sem) = refs[:4], refs[4 : 4 + 2 * zn], refs[4 + 2 * zn :]
    ffw, tok = srcs[0].shape[1:]
    copies = []
    for part in range(2):
        for core in range(2):
            for k in range(top):
                copies.append(
                    pltpu.make_async_copy(
                        srcs[2 * core + part].at[k],
                        cat.at[pl.ds(part * ffw, ffw), pl.ds((2 * k + core) * tok, tok)],
                        sem.at[len(copies)],
                    )
                )
    for copy in copies:
        copy.start()
    z, x, c = sc[0], sc[1], sc[2]
    q = lax.broadcasted_iota(jnp.int32, (2 * zn, 1), 0)
    plane = z + lax.shift_right_logical(q, 1)
    plane = jnp.where(plane >= zn, plane - zn, plane)
    experts = (plane * 4 + lax.bitwise_and(x + q, 1) * 2 + c).astype(F32)
    own = meta_own[...].astype(F32)
    sib = meta_sib[...].astype(F32)
    base = q.astype(F32) * chip_rows + 1.0
    before = before_matrix(tok)
    hits = [[jnp.where(m[k : k + 1] == experts, 1.0, 0.0) for k in range(top)] for m in (own, sib)]
    mask = [sum(h) for h in hits]
    total = [jnp.sum(m, axis=1, keepdims=True) for m in mask]
    core_f = c.astype(F32)
    slot = [dot(m.astype(BF16), before) for m in mask]
    slot = [slot[0] + core_f * total[1] + base, slot[1] + (1.0 - core_f) * total[0] + base]
    targets = []
    for k in range(top):
        for core in range(2):
            targets.append(jnp.sum(hits[core][k] * slot[core], axis=0, keepdims=True) - 1.0)
    target = jnp.concatenate(targets, axis=1)
    for copy in copies:
        copy.wait()
    table = cat[...]
    for j in range(zn):
        row = lax.broadcasted_iota(jnp.int32, (2 * chip_rows, target.shape[1]), 0) + 2 * j * chip_rows
        pick = jnp.where(row.astype(F32) == target, 1.0, 0.0).astype(BF16)
        packed = lax.dot_general(pick, table, NT, preferred_element_type=F32)
        outs[2 * j][...] = packed[:chip_rows].astype(BF16)
        outs[2 * j + 1][...] = packed[chip_rows:].astype(BF16)


def expert_kernel(
    zn, nb, top, chip_rows, j, sc, meta, d00, d01, d10, d11, pre0, pre1, w_gate, w_up, w_down,
    grads_out, hidden_out, rows_out, back0, back1,
):
    z, x, c, g = sc[0], sc[1], sc[2], sc[3]
    expert = (z * 4 + x * 2 + c).astype(F32)
    source = z - j + jnp.where(z < j, zn, 0)
    before = before_matrix(d00.shape[0])
    picked, weights = [], []
    for xr, (own_ref, sib_ref) in enumerate(((d00, d01), (d10, d11))):
        at = g * nb + source * 4 + lax.bitwise_and(x + xr, 1) * 2
        own, own_gate = expert_hits(meta[at + c].astype(F32), top, expert)
        sib, sib_gate = expert_hits(meta[at + 1 - c].astype(F32), top, expert)
        slot = jnp.concatenate(chip_slots(own, sib, c, before), axis=1)
        pick = slot_rows(slot, chip_rows)
        gates = jnp.concatenate([own_gate, sib_gate], axis=1)
        weights.append(jnp.sum(pick * gates, axis=1, keepdims=True))
        both = jnp.concatenate([own_ref[...], sib_ref[...]], axis=0)
        picked.append(dot(pick.astype(BF16), both))
    weight = jnp.concatenate(weights, axis=0)
    rows = jnp.concatenate(picked, axis=0).astype(BF16)
    rows_out[...] = rows
    ffw = w_down.shape[0]
    down = w_down[...]
    back = lax.dot_general(rows, jnp.concatenate([down, down], axis=0), NT, preferred_element_type=F32)
    pre = jnp.concatenate([pre0[...].astype(F32), pre1[...].astype(F32)], axis=0)
    swapped = pltpu.roll(pre, ffw, axis=1)
    first = lax.broadcasted_iota(jnp.int32, pre.shape, 1) < ffw
    gate_pre = jnp.where(first, pre, swapped)
    up_pre = jnp.where(first, swapped, pre)
    sig = jax.nn.sigmoid(gate_pre)
    active = gate_pre * sig
    slope = jnp.where(first, up_pre * sig * (1.0 + gate_pre * (1.0 - sig)), active)
    grads = (weight * back * slope).astype(BF16)
    grads_out[...] = grads
    hidden_out[...] = (weight * active * up_pre)[:, :ffw].astype(BF16)
    route = dot(grads, jnp.concatenate([w_gate[...], w_up[...]], axis=0))
    back0[...] = route[:chip_rows].astype(BF16)
    back1[...] = route[chip_rows:].astype(BF16)


def combine_kernel(zn, nb, top, chip_rows, j, sc, meta, r00, r01, r10, r11, out):
    z, x, c, g = sc[0], sc[1], sc[2], sc[3]
    source = z - j + jnp.where(z < j, zn, 0)
    at = g * nb + source * 4 + x * 2
    own_meta = meta[at + c].astype(F32)
    sib_meta = meta[at + 1 - c].astype(F32)
    before = before_matrix(out.shape[0])
    total = jnp.zeros(out.shape, F32)
    for n, ref in enumerate((r00, r01, r10, r11)):
        xr, cr = n // 2, n % 2
        expert = z * 4 + lax.bitwise_and(x + xr, 1) * 2 + lax.bitwise_and(c + cr, 1)
        own, _ = expert_hits(own_meta, top, expert.astype(F32))
        sib, _ = expert_hits(sib_meta, top, expert.astype(F32))
        slot, _ = chip_slots(own, sib, c, before)
        pick = slot_rows(slot, chip_rows).astype(BF16)
        total = total + lax.dot_general(pick, ref[...], TN, preferred_element_type=F32)
    out[...] = total.astype(BF16)


def inner_kernel(zn, nb, ng, top, chip_rows, sc, meta, *refs):
    n_x, n_g = 4 * zn, zn * ng
    xs, gs = refs[:n_x], refs[n_x : n_x + n_g]
    gate_out, up_out, table, grads, grads_t, rows, sem_x, sem_g = refs[n_x + n_g :]
    tok = xs[0].shape[0] // ng
    ffw, width = gate_out.shape
    quad = 2 * chip_rows
    copies = []
    for j in range(zn):
        for n in range(4):
            for r in range(ng):
                copies.append(
                    pltpu.make_async_copy(
                        xs[4 * j + n].at[pl.ds(r * tok, tok)],
                        table.at[j * ng + r, n // 2, pl.ds((n % 2) * tok, tok)],
                        sem_x.at[len(copies)],
                    )
                )
    for u in range(n_g):
        copies.append(pltpu.make_async_copy(gs[u], grads.at[pl.ds(u * quad, quad)], sem_g.at[u]))
    for copy in copies:
        copy.start()
    z, x, c, g = sc[0], sc[1], sc[2], sc[3]
    expert = (z * 4 + x * 2 + c).astype(F32)
    before = before_matrix(tok)
    for copy in copies:
        copy.wait()

    def pick_rows(u, carry):
        j, r = u // ng, u % ng
        source = lax.rem(z - j + zn, zn)
        group = lax.rem(g - r + ng, ng)
        picked = []
        for xr in range(2):
            at = group * nb + source * 4 + lax.bitwise_and(x + xr, 1) * 2
            own, _ = expert_hits(meta[at + c].astype(F32), top, expert)
            sib, _ = expert_hits(meta[at + 1 - c].astype(F32), top, expert)
            slot = jnp.concatenate(chip_slots(own, sib, c, before), axis=1)
            picked.append(dot(slot_rows(slot, chip_rows).astype(BF16), table[u, xr]))
        rows[pl.ds(pl.multiple_of(u * quad, 16), quad), :] = jnp.concatenate(picked, axis=0).astype(BF16)
        return carry

    lax.fori_loop(0, n_g, pick_rows, 0)
    total = n_g * quad
    step = 128
    for i in range(0, total, step):
        grads_t[:, i : i + step] = grads[i : i + step, :].T
    chunk = min(256, width)

    def product(n, carry):
        cols = pl.ds(pl.multiple_of(n * chunk, chunk), chunk)
        both = dot(grads_t[...], rows[:, cols])
        gate_out[:, cols] = both[:ffw].astype(BF16)
        up_out[:, cols] = both[ffw:].astype(BF16)
        return carry

    lax.fori_loop(0, width // chunk, product, 0)


def outer_kernel(zn, ng, sc, *refs):
    hs, ds = refs[:zn], refs[zn : 2 * zn]
    own, sent, hidden, rows, sem = refs[2 * zn :]
    quad = hs[0].shape[0]
    copies = []
    for j in range(zn):
        copies.append(pltpu.make_async_copy(hs[j], hidden.at[pl.ds(j * quad, quad)], sem.at[2 * j]))
        copies.append(pltpu.make_async_copy(ds[j], rows.at[pl.ds(j * quad, quad)], sem.at[2 * j + 1]))
    for copy in copies:
        copy.start()
    for copy in copies:
        copy.wait()
    g = sc[3]
    width = own.shape[1]
    chunk = min(256, width)
    hidden_t = hidden[...].T

    for r in range(ng):
        base = lax.rem(g + r, ng) * width

        def product(n, carry):
            cols = pl.ds(pl.multiple_of(base + n * chunk, chunk), chunk)
            value = dot(hidden_t, rows[:, cols])
            to = pl.ds(pl.multiple_of(n * chunk, chunk), chunk)
            if r == 0:
                own[:, to] = value
            else:
                sent[r - 1, :, to] = value.astype(BF16)
            return carry

        lax.fori_loop(0, width // chunk, product, 0)


def per_device(
    tokens, d_out, expert_ids, gate_values, saved_gate_pre, saved_up_pre, w_gate, w_up, w_down
):
    tok, width = tokens.shape
    top = expert_ids.shape[1]
    ffw = saved_gate_pre.shape[2]
    nb, ng = lax.axis_size("blk"), lax.axis_size("grp")
    zn = nb // 4
    experts = w_gate.shape[0] * nb
    slots = 13 * tok // (2 * experts)
    chip_rows = -(-2 * slots // 8) * 8
    quad = 2 * chip_rows
    part = width // ng
    me, g = lax.axis_index("blk"), lax.axis_index("grp")
    z, x, c = me // 4, (me // 2) % 2, me % 2
    sc = jnp.stack([z, x, c, g]).astype(jnp.int32)

    def shift(value, n):
        return lax.ppermute(value, "blk", [(b, (b + 4 * n) % nb) for b in range(nb)])

    def over_x(value):
        return lax.ppermute(value, "blk", [(b, b ^ 2) for b in range(nb)])

    def over_core(value):
        return lax.ppermute(value, "blk", [(b, b ^ 1) for b in range(nb)])

    def over_groups(value, n):
        return lax.ppermute(value, "grp", [(b, (b + n) % ng) for b in range(ng)])

    def gathered(block):
        out = []
        for j in range(zn):
            if j:
                block = shift(block, 1)
            hop = over_x(block)
            out.append((block, over_core(block), hop, over_core(hop)))
        return out

    smem = pl.BlockSpec(memory_space=pltpu.SMEM)
    vmem = pl.BlockSpec(memory_space=pltpu.VMEM)
    anywhere = pl.BlockSpec(memory_space=pl.ANY)

    def shape(*dims, dtype=BF16):
        return jax.ShapeDtypeStruct(dims, dtype)

    meta = jnp.concatenate([expert_ids.T.astype(BF16), gate_values.T], axis=0)
    meta_all = lax.all_gather(meta, ("grp", "blk"))
    meta_sib = over_core(meta)
    pre = [saved_gate_pre.transpose(1, 2, 0), saved_up_pre.transpose(1, 2, 0)]
    pre_sib = [over_core(p) for p in pre]
    grads_in = gathered(d_out)

    packed = pl.pallas_call(
        functools.partial(pack_kernel, zn, top, chip_rows),
        out_shape=[shape(chip_rows, 2 * ffw)] * (2 * zn),
        in_specs=[smem, vmem, vmem] + [anywhere] * 4,
        out_specs=[vmem] * (2 * zn),
        scratch_shapes=[
            pltpu.VMEM((2 * ffw, 2 * top * tok), BF16),
            pltpu.SemaphoreType.DMA((4 * top,)),
        ],
        compiler_params=params(),
        cost_estimate=cost(2 * zn * quad * 2 * top * tok * 2 * ffw, 8 * top * tok * ffw * 2),
        name="pack",
    )(sc, meta, meta_sib, *pre, *pre_sib)
    arrived = []
    for j in range(zn):
        near, far = packed[2 * j], over_x(packed[2 * j + 1])
        arrived.append((shift(near, j), shift(far, j)) if j else (near, far))

    weights = (w_gate[0].T, w_up[0].T, w_down[0])
    done = []
    for j in range(zn):
        done.append(
            pl.pallas_call(
                functools.partial(expert_kernel, zn, nb, top, chip_rows, j),
                out_shape=[
                    shape(quad, 2 * ffw),
                    shape(quad, ffw),
                    shape(quad, width),
                    shape(chip_rows, width),
                    shape(chip_rows, width),
                ],
                in_specs=[smem] + [vmem] * 10,
                out_specs=[vmem] * 5,
                compiler_params=params(),
                cost_estimate=cost(2 * quad * width * ffw * 4 + 2 * quad * tok * 2 * width, 16e6),
                name="expert",
            )(sc, meta_all, *grads_in[j], *arrived[j], *weights)
        )

    partials = []
    for j in range(zn):
        near, far = done[j][3], over_x(done[j][4])
        partials.append(
            pl.pallas_call(
                functools.partial(combine_kernel, zn, nb, top, chip_rows, j),
                out_shape=shape(tok, width),
                in_specs=[smem] + [vmem] * 5,
                out_specs=vmem,
                compiler_params=params(),
                cost_estimate=cost(2 * 4 * tok * chip_rows * width, 3e6),
                name="combine",
            )(sc, meta_all, near, over_core(near), far, over_core(far))
        )
    d_tokens = partials[0].astype(F32)
    for j in range(1, zn):
        d_tokens = d_tokens + shift(partials[j], -j).astype(F32)

    down_own, down_sent = pl.pallas_call(
        functools.partial(outer_kernel, zn, ng),
        out_shape=[shape(ffw, part, dtype=F32), shape(max(ng - 1, 1), ffw, part)],
        in_specs=[smem] + [anywhere] * (2 * zn),
        out_specs=[vmem, vmem],
        scratch_shapes=[
            pltpu.VMEM((zn * quad, ffw), BF16),
            pltpu.VMEM((zn * quad, width), BF16),
            pltpu.SemaphoreType.DMA((2 * zn,)),
        ],
        compiler_params=params(),
        cost_estimate=cost(2 * zn * quad * ffw * width, 10e6),
        name="outer",
    )(sc, *[d[1] for d in done], *[d[2] for d in done])
    d_down = down_own
    for r in range(1, ng):
        d_down = d_down + over_groups(down_sent[r - 1], r).astype(F32)

    own_part = lax.dynamic_slice(tokens, (0, g * part), (tok, part))
    pieces = [own_part]
    for r in range(1, ng):
        there = lax.dynamic_slice(tokens, (0, ((g + r) % ng) * part), (tok, part))
        pieces.append(over_groups(there, r))
    inputs = gathered(jnp.concatenate(pieces, axis=0))
    grads = []
    for j in range(zn):
        grads.append(done[j][0])
        for r in range(1, ng):
            grads.append(over_groups(done[j][0], r))
    units = zn * ng
    d_gate, d_up = pl.pallas_call(
        functools.partial(inner_kernel, zn, nb, ng, top, chip_rows),
        out_shape=[shape(ffw, part)] * 2,
        in_specs=[smem, vmem] + [anywhere] * (4 * zn + units),
        out_specs=[vmem, vmem],
        scratch_shapes=[
            pltpu.VMEM((units, 2, 2 * tok, part), BF16),
            pltpu.VMEM((units * quad, 2 * ffw), BF16),
            pltpu.VMEM((2 * ffw, units * quad), BF16),
            pltpu.VMEM((units * quad, part), BF16),
            pltpu.SemaphoreType.DMA((4 * units,)),
            pltpu.SemaphoreType.DMA((units,)),
        ],
        compiler_params=params(),
        cost_estimate=cost(2 * units * quad * 2 * ffw * part, 20e6),
        name="inner",
    )(sc, meta_all, *[block for plane in inputs for block in plane], *grads)
    return (
        d_tokens.astype(BF16),
        d_gate.T[None],
        d_up.T[None],
        d_down.astype(BF16)[None],
    )


def solution(mesh):
    return jax.shard_map(
        per_device,
        mesh=mesh,
        in_specs=(
            P(("grp", "blk"), None),
            P(("grp", "blk"), None),
            P(("grp", "blk"), None),
            P(("grp", "blk"), None),
            P(("grp", "blk"), None, None),
            P(("grp", "blk"), None, None),
            P("blk", None, None),
            P("blk", None, None),
            P("blk", None, None),
        ),
        out_specs=(
            P(("grp", "blk"), None),
            P("blk", "grp", None),
            P("blk", "grp", None),
            P("blk", None, "grp"),
        ),
        check_vma=False,
    )
```

```python
import functools

import jax
import jax.numpy as jnp
from jax import lax
from jax.experimental import pallas as pl
from jax.experimental.pallas import tpu as pltpu
from jax.sharding import PartitionSpec as P

BF16 = jnp.bfloat16
F32 = jnp.float32
MIB = 1024 * 1024
NT = (((1,), (1,)), ((), ()))
TN = (((0,), (0,)), ((), ()))


def params(mib):
    return pltpu.CompilerParams(vmem_limit_bytes=mib * MIB)


def cost(flops, moved):
    return pl.CostEstimate(flops=int(flops), bytes_accessed=int(moved), transcendentals=0)


def dot(a, b):
    return jnp.dot(a, b, preferred_element_type=F32)


def before_matrix(size):
    row = lax.broadcasted_iota(jnp.int32, (size, size), 0)
    col = lax.broadcasted_iota(jnp.int32, (size, size), 1)
    return jnp.where(row < col, 1.0, 0.0).astype(BF16)


def expert_hits(meta, top, expert):
    hits = jnp.where(meta[:top] == expert, 1.0, 0.0)
    return jnp.sum(hits, axis=0, keepdims=True), jnp.sum(hits * meta[top:], axis=0, keepdims=True)


def chip_slots(own, sib, core, before):
    rows = jnp.broadcast_to(own, (8, own.shape[1])), jnp.broadcast_to(sib, (8, sib.shape[1]))
    own_before = dot(rows[0].astype(BF16), before)[:1]
    sib_before = dot(rows[1].astype(BF16), before)[:1]
    own_total = jnp.sum(own, axis=1, keepdims=True)
    sib_total = jnp.sum(sib, axis=1, keepdims=True)
    core_f = core.astype(F32)
    own_slot = jnp.where(own > 0, own_before + core_f * sib_total, -1.0)
    sib_slot = jnp.where(sib > 0, sib_before + (1.0 - core_f) * own_total, -1.0)
    return own_slot, sib_slot


def slot_rows(slot, count):
    row = lax.broadcasted_iota(jnp.int32, (count, slot.shape[1]), 0).astype(F32)
    return jnp.where(row == slot, 1.0, 0.0)


def pack_kernel(zn, top, chip_rows, sc, meta_own, meta_sib, *refs):
    srcs, outs, (cat, sem) = refs[:4], refs[4 : 4 + 2 * zn], refs[4 + 2 * zn :]
    ffw, tok = srcs[0].shape[1:]
    copies = []
    for part in range(2):
        for core in range(2):
            for k in range(top):
                copies.append(
                    pltpu.make_async_copy(
                        srcs[2 * core + part].at[k],
                        cat.at[pl.ds(part * ffw, ffw), pl.ds((2 * k + core) * tok, tok)],
                        sem.at[len(copies)],
                    )
                )
    for copy in copies:
        copy.start()
    z, x, c = sc[0], sc[1], sc[2]
    q = lax.broadcasted_iota(jnp.int32, (2 * zn, 1), 0)
    plane = z + lax.shift_right_logical(q, 1)
    plane = jnp.where(plane >= zn, plane - zn, plane)
    experts = (plane * 4 + lax.bitwise_and(x + q, 1) * 2 + c).astype(F32)
    own = meta_own[...].astype(F32)
    sib = meta_sib[...].astype(F32)
    base = q.astype(F32) * chip_rows + 1.0
    before = before_matrix(tok)
    hits = [[jnp.where(m[k : k + 1] == experts, 1.0, 0.0) for k in range(top)] for m in (own, sib)]
    mask = [sum(h) for h in hits]
    total = [jnp.sum(m, axis=1, keepdims=True) for m in mask]
    core_f = c.astype(F32)
    slot = [dot(m.astype(BF16), before) for m in mask]
    slot = [slot[0] + core_f * total[1] + base, slot[1] + (1.0 - core_f) * total[0] + base]
    targets = []
    for k in range(top):
        for core in range(2):
            targets.append(jnp.sum(hits[core][k] * slot[core], axis=0, keepdims=True) - 1.0)
    target = jnp.concatenate(targets, axis=1)
    for copy in copies:
        copy.wait()
    table = cat[...]
    for j in range(zn):
        row = lax.broadcasted_iota(jnp.int32, (2 * chip_rows, target.shape[1]), 0) + 2 * j * chip_rows
        pick = jnp.where(row.astype(F32) == target, 1.0, 0.0).astype(BF16)
        packed = lax.dot_general(pick, table, NT, preferred_element_type=F32)
        outs[2 * j][...] = packed[:chip_rows].astype(BF16)
        outs[2 * j + 1][...] = packed[chip_rows:].astype(BF16)


def expert_kernel(
    top, chip_rows, sc, meta, d00, d01, d10, d11, pre0, pre1, w_gate, w_up, w_down,
    grads_out, hidden_out, rows_out, back0, back1, down_at, both_at, sem,
):
    z, x, c = sc[0], sc[1], sc[2]
    ffw = w_down.shape[0]
    copies = [
        pltpu.make_async_copy(w_down, down_at.at[pl.ds(0, ffw)], sem.at[0]),
        pltpu.make_async_copy(w_down, down_at.at[pl.ds(ffw, ffw)], sem.at[1]),
        pltpu.make_async_copy(w_gate, both_at.at[pl.ds(0, ffw)], sem.at[2]),
        pltpu.make_async_copy(w_up, both_at.at[pl.ds(ffw, ffw)], sem.at[3]),
    ]
    for copy in copies:
        copy.start()
    expert = (z * 4 + x * 2 + c).astype(F32)
    before = before_matrix(d00.shape[0])
    picked, weights = [], []
    for xr, (own_ref, sib_ref) in enumerate(((d00, d01), (d10, d11))):
        own, own_gate = expert_hits(meta[0, xr, 0].astype(F32), top, expert)
        sib, sib_gate = expert_hits(meta[0, xr, 1].astype(F32), top, expert)
        slot = jnp.concatenate(chip_slots(own, sib, c, before), axis=1)
        pick = slot_rows(slot, chip_rows)
        gates = jnp.concatenate([own_gate, sib_gate], axis=1)
        weights.append(jnp.sum(pick * gates, axis=1, keepdims=True))
        both = jnp.concatenate([own_ref[...], sib_ref[...]], axis=0)
        picked.append(dot(pick.astype(BF16), both))
    weight = jnp.concatenate(weights, axis=0)
    rows = jnp.concatenate(picked, axis=0).astype(BF16)
    rows_out[...] = rows
    copies[0].wait()
    copies[1].wait()
    back = lax.dot_general(rows, down_at[...], NT, preferred_element_type=F32)
    pre = jnp.concatenate([pre0[...].astype(F32), pre1[...].astype(F32)], axis=0)
    swapped = pltpu.roll(pre, ffw, axis=1)
    first = lax.broadcasted_iota(jnp.int32, pre.shape, 1) < ffw
    gate_pre = jnp.where(first, pre, swapped)
    up_pre = jnp.where(first, swapped, pre)
    sig = jax.nn.sigmoid(gate_pre)
    active = gate_pre * sig
    slope = jnp.where(first, up_pre * sig * (1.0 + gate_pre * (1.0 - sig)), active)
    grads = (weight * back * slope).astype(BF16)
    grads_out[...] = grads
    hidden_out[...] = (weight * active * up_pre)[:, :ffw].astype(BF16)
    copies[2].wait()
    copies[3].wait()
    route = dot(grads, both_at[...])
    back0[...] = route[:chip_rows].astype(BF16)
    back1[...] = route[chip_rows:].astype(BF16)


def combine_kernel(top, chip_rows, sc, meta, r00, r01, r10, r11, out):
    z, x, c = sc[0], sc[1], sc[2]
    own_meta = meta[0, 0, 0].astype(F32)
    sib_meta = meta[0, 0, 1].astype(F32)
    before = before_matrix(out.shape[0])
    total = jnp.zeros(out.shape, F32)
    for n, ref in enumerate((r00, r01, r10, r11)):
        xr, cr = n // 2, n % 2
        expert = z * 4 + lax.bitwise_and(x + xr, 1) * 2 + lax.bitwise_and(c + cr, 1)
        own, _ = expert_hits(own_meta, top, expert.astype(F32))
        sib, _ = expert_hits(sib_meta, top, expert.astype(F32))
        slot, _ = chip_slots(own, sib, c, before)
        pick = slot_rows(slot, chip_rows).astype(BF16)
        total = total + lax.dot_general(pick, ref[...], TN, preferred_element_type=F32)
    out[...] = total.astype(BF16)


def inner_kernel(zn, ng, top, chip_rows, sc, *refs):
    n_x, n_g = 4 * zn, zn * ng
    metas, xs, gs = refs[:zn], refs[zn : zn + n_x], refs[zn + n_x : zn + n_x + n_g]
    gate_out, up_out, table, grads, grads_t, rows, sem_x, sem_g = refs[zn + n_x + n_g :]
    tok = xs[0].shape[0] // ng
    ffw, width = gate_out.shape
    quad = 2 * chip_rows
    copies = []
    for u in range(n_g):
        j, r = u // ng, u % ng
        mine = [
            pltpu.make_async_copy(
                xs[4 * j + n].at[pl.ds(r * tok, tok)],
                table.at[u, n // 2, pl.ds((n % 2) * tok, tok)],
                sem_x.at[4 * u + n],
            )
            for n in range(4)
        ]
        mine.append(pltpu.make_async_copy(gs[u], grads.at[pl.ds(u * quad, quad)], sem_g.at[u]))
        copies.append(mine)
        for copy in mine:
            copy.start()
    z, x, c = sc[0], sc[1], sc[2]
    expert = (z * 4 + x * 2 + c).astype(F32)
    before = before_matrix(tok)
    for u in range(n_g):
        j, r = u // ng, u % ng
        picks = []
        for xr in range(2):
            own, _ = expert_hits(metas[j][r, xr, 0].astype(F32), top, expert)
            sib, _ = expert_hits(metas[j][r, xr, 1].astype(F32), top, expert)
            slot = jnp.concatenate(chip_slots(own, sib, c, before), axis=1)
            picks.append(slot_rows(slot, chip_rows).astype(BF16))
        for copy in copies[u]:
            copy.wait()
        picked = [dot(pick, table[u, xr]) for xr, pick in enumerate(picks)]
        rows[u * quad : (u + 1) * quad, :] = jnp.concatenate(picked, axis=0).astype(BF16)
    total = n_g * quad
    step = 128
    for i in range(0, total, step):
        grads_t[:, i : i + step] = grads[i : i + step, :].T
    chunk = min(256, width)

    def product(n, carry):
        cols = pl.ds(pl.multiple_of(n * chunk, chunk), chunk)
        both = dot(grads_t[...], rows[:, cols])
        gate_out[:, cols] = both[:ffw].astype(BF16)
        up_out[:, cols] = both[ffw:].astype(BF16)
        return carry

    lax.fori_loop(0, width // chunk, product, 0)


def outer_kernel(zn, ng, sc, *refs):
    hs, ds = refs[:zn], refs[zn : 2 * zn]
    own, sent, hidden, rows, sem = refs[2 * zn :]
    quad = hs[0].shape[0]
    copies = []
    for j in range(zn):
        copies.append(pltpu.make_async_copy(hs[j], hidden.at[pl.ds(j * quad, quad)], sem.at[2 * j]))
        copies.append(pltpu.make_async_copy(ds[j], rows.at[pl.ds(j * quad, quad)], sem.at[2 * j + 1]))
    for copy in copies:
        copy.start()
    for copy in copies:
        copy.wait()
    g = sc[3]
    width = own.shape[1]
    chunk = min(256, width)
    hidden_t = hidden[...].T

    for r in range(ng):
        base = lax.rem(g + r, ng) * width

        def product(n, carry):
            cols = pl.ds(pl.multiple_of(base + n * chunk, chunk), chunk)
            value = dot(hidden_t, rows[:, cols])
            to = pl.ds(pl.multiple_of(n * chunk, chunk), chunk)
            if r == 0:
                own[:, to] = value
            else:
                sent[r - 1, :, to] = value.astype(BF16)
            return carry

        lax.fori_loop(0, width // chunk, product, 0)


def per_device(
    tokens, d_out, expert_ids, gate_values, saved_gate_pre, saved_up_pre, w_gate, w_up, w_down
):
    tok, width = tokens.shape
    top = expert_ids.shape[1]
    ffw = saved_gate_pre.shape[2]
    nb, ng = lax.axis_size("blk"), lax.axis_size("grp")
    zn = nb // 4
    experts = w_gate.shape[0] * nb
    slots = 13 * tok // (2 * experts)
    chip_rows = -(-2 * slots // 8) * 8
    quad = 2 * chip_rows
    part = width // ng
    me, g = lax.axis_index("blk"), lax.axis_index("grp")
    z, x, c = me // 4, (me // 2) % 2, me % 2
    sc = jnp.stack([z, x, c, g]).astype(jnp.int32)

    def shift(value, n):
        return lax.ppermute(value, "blk", [(b, (b + 4 * n) % nb) for b in range(nb)])

    def over_x(value):
        return lax.ppermute(value, "blk", [(b, b ^ 2) for b in range(nb)])

    def over_core(value):
        return lax.ppermute(value, "blk", [(b, b ^ 1) for b in range(nb)])

    def over_groups(value, n):
        return lax.ppermute(value, "grp", [(b, (b + n) % ng) for b in range(ng)])

    def gathered(block):
        out = []
        for j in range(zn):
            if j:
                block = shift(block, 1)
            hop = over_x(block)
            out.append((block, over_core(block), hop, over_core(hop)))
        return out

    smem = pl.BlockSpec(memory_space=pltpu.SMEM)
    vmem = pl.BlockSpec(memory_space=pltpu.VMEM)
    anywhere = pl.BlockSpec(memory_space=pl.ANY)

    def shape(*dims, dtype=BF16):
        return jax.ShapeDtypeStruct(dims, dtype)

    meta = jnp.concatenate([expert_ids.T.astype(BF16), gate_values.T], axis=0)
    meta_sib = over_core(meta)
    chip_meta = jnp.stack([meta, meta_sib])
    plane_meta = jnp.stack([chip_meta, over_x(chip_meta)])
    all_meta = jnp.stack([plane_meta] + [over_groups(plane_meta, r) for r in range(1, ng)])
    metas = [all_meta] + [shift(all_meta, j) for j in range(1, zn)]
    pre = [saved_gate_pre.transpose(1, 2, 0), saved_up_pre.transpose(1, 2, 0)]
    pre_sib = [over_core(p) for p in pre]
    grads_in = gathered(d_out)

    packed = pl.pallas_call(
        functools.partial(pack_kernel, zn, top, chip_rows),
        out_shape=[shape(chip_rows, 2 * ffw)] * (2 * zn),
        in_specs=[smem, vmem, vmem] + [anywhere] * 4,
        out_specs=[vmem] * (2 * zn),
        scratch_shapes=[
            pltpu.VMEM((2 * ffw, 2 * top * tok), BF16),
            pltpu.SemaphoreType.DMA((4 * top,)),
        ],
        compiler_params=params(24),
        cost_estimate=cost(2 * zn * quad * 2 * top * tok * 2 * ffw, 8 * top * tok * ffw * 2),
        name="pack",
    )(sc, meta, meta_sib, *pre, *pre_sib)
    arrived = []
    for j in range(zn):
        near, far = packed[2 * j], over_x(packed[2 * j + 1])
        arrived.append((shift(near, j), shift(far, j)) if j else (near, far))

    weights = (w_gate[0].T, w_up[0].T, w_down[0])
    done = []
    for j in range(zn):
        done.append(
            pl.pallas_call(
                functools.partial(expert_kernel, top, chip_rows),
                out_shape=[
                    shape(quad, 2 * ffw),
                    shape(quad, ffw),
                    shape(quad, width),
                    shape(chip_rows, width),
                    shape(chip_rows, width),
                ],
                in_specs=[smem] + [vmem] * 7 + [anywhere] * 3,
                out_specs=[vmem] * 5,
                scratch_shapes=[
                    pltpu.VMEM((2 * ffw, width), BF16),
                    pltpu.VMEM((2 * ffw, width), BF16),
                    pltpu.SemaphoreType.DMA((4,)),
                ],
                compiler_params=params(32),
                cost_estimate=cost(2 * quad * width * ffw * 4 + 2 * quad * tok * 2 * width, 16e6),
                name="expert",
            )(sc, metas[j], *grads_in[j], *arrived[j], *weights)
        )

    partials = []
    for j in range(zn):
        near, far = done[j][3], over_x(done[j][4])
        partials.append(
            pl.pallas_call(
                functools.partial(combine_kernel, top, chip_rows),
                out_shape=shape(tok, width),
                in_specs=[smem] + [vmem] * 5,
                out_specs=vmem,
                compiler_params=params(12),
                cost_estimate=cost(2 * 4 * tok * chip_rows * width, 3e6),
                name="combine",
            )(sc, metas[j], near, over_core(near), far, over_core(far))
        )
    d_tokens = partials[0].astype(F32)
    for j in range(1, zn):
        d_tokens = d_tokens + shift(partials[j], -j).astype(F32)

    down_own, down_sent = pl.pallas_call(
        functools.partial(outer_kernel, zn, ng),
        out_shape=[shape(ffw, part, dtype=F32), shape(max(ng - 1, 1), ffw, part)],
        in_specs=[smem] + [anywhere] * (2 * zn),
        out_specs=[vmem, vmem],
        scratch_shapes=[
            pltpu.VMEM((zn * quad, ffw), BF16),
            pltpu.VMEM((zn * quad, width), BF16),
            pltpu.SemaphoreType.DMA((2 * zn,)),
        ],
        compiler_params=params(24),
        cost_estimate=cost(2 * zn * quad * ffw * width, 10e6),
        name="outer",
    )(sc, *[d[1] for d in done], *[d[2] for d in done])
    d_down = down_own
    for r in range(1, ng):
        d_down = d_down + over_groups(down_sent[r - 1], r).astype(F32)

    own_part = lax.dynamic_slice(tokens, (0, g * part), (tok, part))
    pieces = [own_part]
    for r in range(1, ng):
        there = lax.dynamic_slice(tokens, (0, ((g + r) % ng) * part), (tok, part))
        pieces.append(over_groups(there, r))
    block, _ = lax.optimization_barrier((jnp.concatenate(pieces, axis=0), packed[0]))
    inputs = gathered(block)
    grads = []
    for j in range(zn):
        grads.append(done[j][0])
        for r in range(1, ng):
            grads.append(over_groups(done[j][0], r))
    units = zn * ng
    d_gate, d_up = pl.pallas_call(
        functools.partial(inner_kernel, zn, ng, top, chip_rows),
        out_shape=[shape(ffw, part)] * 2,
        in_specs=[smem] + [vmem] * zn + [anywhere] * (4 * zn + units),
        out_specs=[vmem, vmem],
        scratch_shapes=[
            pltpu.VMEM((units, 2, 2 * tok, part), BF16),
            pltpu.VMEM((units * quad, 2 * ffw), BF16),
            pltpu.VMEM((2 * ffw, units * quad), BF16),
            pltpu.VMEM((units * quad, part), BF16),
            pltpu.SemaphoreType.DMA((4 * units,)),
            pltpu.SemaphoreType.DMA((units,)),
        ],
        compiler_params=params(40 if units <= 16 else 56),
        cost_estimate=cost(2 * units * quad * 2 * ffw * part, 20e6),
        name="inner",
    )(sc, *metas, *[block for plane in inputs for block in plane], *grads)
    return (
        d_tokens.astype(BF16),
        d_gate.T[None],
        d_up.T[None],
        d_down.astype(BF16)[None],
    )


def solution(mesh):
    return jax.shard_map(
        per_device,
        mesh=mesh,
        in_specs=(
            P(("grp", "blk"), None),
            P(("grp", "blk"), None),
            P(("grp", "blk"), None),
            P(("grp", "blk"), None),
            P(("grp", "blk"), None, None),
            P(("grp", "blk"), None, None),
            P("blk", None, None),
            P("blk", None, None),
            P("blk", None, None),
        ),
        out_specs=(
            P(("grp", "blk"), None),
            P("blk", "grp", None),
            P("blk", "grp", None),
            P("blk", None, "grp"),
        ),
        check_vma=False,
    )
```

```python
import functools

import jax
import jax.numpy as jnp
from jax import lax
from jax.experimental import pallas as pl
from jax.experimental.pallas import tpu as pltpu
from jax.sharding import PartitionSpec as P

BF16 = jnp.bfloat16
F32 = jnp.float32
MIB = 1024 * 1024
PACK, EXPERT, COMBINE, OUTER, INNER = 24, 40, 12, 24, 40
NT = (((1,), (1,)), ((), ()))
TN = (((0,), (0,)), ((), ()))


def params(mib):
    return pltpu.CompilerParams(vmem_limit_bytes=mib * MIB)


def cost(flops, moved):
    return pl.CostEstimate(flops=int(flops), bytes_accessed=int(moved), transcendentals=0)


def dot(a, b):
    return jnp.dot(a, b, preferred_element_type=F32)


def before_matrix(size):
    row = lax.broadcasted_iota(jnp.int32, (size, size), 0)
    col = lax.broadcasted_iota(jnp.int32, (size, size), 1)
    return jnp.where(row < col, 1.0, 0.0).astype(BF16)


def slot_rows(slot, count):
    row = lax.broadcasted_iota(jnp.int32, (count, slot.shape[1]), 0).astype(F32)
    return jnp.where(row == slot, 1.0, 0.0)


def moved(slot, by):
    return jnp.where(slot < 0, -1.0, slot + by)


def with_notes(rows, notes, slots, block):
    count, lanes = rows.shape[0], notes[0].shape[1]
    row = lax.rem(lax.broadcasted_iota(jnp.int32, (count, lanes), 0), block)
    spread = jnp.concatenate([jnp.broadcast_to(note, (block, lanes)) for note in notes], axis=0)
    return jnp.concatenate([jnp.where(row >= slots, spread, rows[:, :lanes]), rows[:, lanes:]], axis=1)


def pack_kernel(top, slots, block, sc, meta_ref, gate_pre, up_pre, keep, swap, cat, sem):
    ffw, tok = gate_pre.shape[1:]
    copies = []
    for part, src in enumerate((gate_pre, up_pre)):
        for k in range(top):
            copies.append(
                pltpu.make_async_copy(
                    src.at[k],
                    cat.at[pl.ds(part * ffw, ffw), pl.ds(k * tok, tok)],
                    sem.at[len(copies)],
                )
            )
    for copy in copies:
        copy.start()
    zn = keep.shape[0]
    experts = 4 * zn
    meta = meta_ref[...].astype(F32)
    order = lax.broadcasted_iota(jnp.int32, (experts, 1), 0)

    def turned(value, by):
        return lax.bitwise_xor(value, jnp.broadcast_to(by, value.shape))

    here = sc[0] * 4 + sc[1] * 2 + sc[2]
    across = jnp.where(order >= 2 * zn, 1, 0)
    expert = turned(lax.bitwise_and(order, 2 * zn - 1) * 2 + across, here).astype(F32)
    hits = [jnp.where(meta[k : k + 1] == expert, 1.0, 0.0) for k in range(top)]
    mask = sum(hits)
    slot = dot(mask.astype(BF16), before_matrix(tok))
    gates = sum(hits[k] * meta[top + k : top + k + 1] for k in range(top))
    notes = jnp.concatenate([jnp.where(mask > 0, slot, -1.0), gates], axis=1)
    place = slot + order.astype(F32) * block + 1.0
    target = jnp.concatenate(
        [jnp.sum(hits[k] * place, axis=0, keepdims=True) - 1.0 for k in range(top)], axis=1
    )
    for copy in copies:
        copy.wait()
    table = cat[...]
    lot = 4
    for first in range(0, experts, lot):
        pick = slot_rows(moved(target, -float(first * block)), lot * block).astype(BF16)
        packed = lax.dot_general(pick, table, NT, preferred_element_type=F32)
        packed = with_notes(packed, [notes[first + n : first + n + 1] for n in range(lot)], slots, block)
        for n in range(lot):
            at = (first + n) % (2 * zn)
            out = keep if first + n < 2 * zn else swap
            out[at // 2, at % 2] = packed[n * block : (n + 1) * block].astype(BF16)


def expert_kernel(
    slots, block, d00, d01, d10, d11, near, far, w_gate, w_up, w_down,
    grads_out, hidden_out, rows_out, keep_out, swap_out, hop_out, down_at, both_at, sem,
):
    ffw = w_down.shape[0]
    copies = [
        pltpu.make_async_copy(w_down, down_at.at[pl.ds(0, ffw)], sem.at[0]),
        pltpu.make_async_copy(w_down, down_at.at[pl.ds(ffw, ffw)], sem.at[1]),
        pltpu.make_async_copy(w_gate, both_at.at[pl.ds(0, ffw)], sem.at[2]),
        pltpu.make_async_copy(w_up, both_at.at[pl.ds(ffw, ffw)], sem.at[3]),
    ]
    for copy in copies:
        copy.start()
    tok = d00.shape[0]
    quad = 4 * block
    pre = jnp.concatenate([near[...].astype(F32), far[...].astype(F32)], axis=0)
    notes = [pre[n * block + slots : n * block + slots + 1, : 2 * tok] for n in range(4)]
    target = jnp.concatenate([moved(note[:, :tok], float(n * block)) for n, note in enumerate(notes)], axis=1)
    gates = jnp.concatenate([note[:, tok:] for note in notes], axis=1)
    pick = slot_rows(target, quad)
    weight = jnp.sum(pick * gates, axis=1, keepdims=True)
    table = jnp.concatenate([ref[...] for ref in (d00, d01, d10, d11)], axis=0)
    rows = dot(pick.astype(BF16), table).astype(BF16)
    rows_out[...] = rows
    copies[0].wait()
    copies[1].wait()
    back = lax.dot_general(rows, down_at[...], NT, preferred_element_type=F32)
    swapped = pltpu.roll(pre, ffw, axis=1)
    front = lax.broadcasted_iota(jnp.int32, pre.shape, 1) < ffw
    gate_pre = jnp.where(front, pre, swapped)
    up_pre = jnp.where(front, swapped, pre)
    sig = jax.nn.sigmoid(gate_pre)
    active = gate_pre * sig
    slope = jnp.where(front, up_pre * sig * (1.0 + gate_pre * (1.0 - sig)), active)
    grads = weight * back * slope
    hidden_out[...] = (weight * active * up_pre)[:, :ffw].astype(BF16)
    grads_out[...] = with_notes(grads, notes, slots, block).astype(BF16)
    copies[2].wait()
    copies[3].wait()
    route = with_notes(dot(grads.astype(BF16), both_at[...]), notes, slots, block).astype(BF16)
    keep_out[...] = route[:block]
    swap_out[...] = route[block : 2 * block]
    hop_out[...] = route[2 * block :]


def combine_kernel(slots, block, keep, swap, hop, hop_swap, out):
    tok = out.shape[0]
    total = jnp.zeros(out.shape, F32)
    for ref, start in ((keep, 0), (swap, 0), (hop, 0), (hop_swap, block)):
        rows = ref[...].astype(F32)
        slot = moved(rows[start + slots : start + slots + 1, :tok], float(start))
        pick = slot_rows(slot, rows.shape[0]).astype(BF16)
        total = total + lax.dot_general(pick, ref[...], TN, preferred_element_type=F32)
    out[...] = total.astype(BF16)


def inner_kernel(zn, ng, slots, block, *refs):
    n_x, n_g = 4 * zn, zn * ng
    xs, gs = refs[:n_x], refs[n_x : n_x + n_g]
    gate_out, up_out, table, grads, grads_t, rows, sem_x, sem_g = refs[n_x + n_g :]
    tok = xs[0].shape[0] // ng
    ffw, width = gate_out.shape
    quad = 4 * block
    units = n_g
    copies = []
    for u in range(units):
        j, r = u // ng, u % ng
        mine = [pltpu.make_async_copy(gs[u], grads.at[pl.ds(u * quad, quad)], sem_g.at[u])]
        for n in range(4):
            mine.append(
                pltpu.make_async_copy(
                    xs[4 * j + n].at[pl.ds(r * tok, tok)],
                    table.at[u, pl.ds(n * tok, tok)],
                    sem_x.at[4 * u + n],
                )
            )
        copies.append(mine)
        for copy in mine:
            copy.start()
    for u in range(units):
        for copy in copies[u]:
            copy.wait()
        targets = []
        for n in range(4):
            row = n * block + slots
            near = u * quad + row // 16 * 16
            note = grads[near : near + 16, :tok].astype(F32)[row % 16 : row % 16 + 1]
            targets.append(moved(note, float(n * block)))
        pick = slot_rows(jnp.concatenate(targets, axis=1), quad).astype(BF16)
        rows[u * quad : (u + 1) * quad, :] = dot(pick, table[u]).astype(BF16)
    total = units * quad
    step = 128
    for i in range(0, total, step):
        grads_t[:, i : i + step] = grads[i : i + step, :].T
    chunk = min(256, width)

    def product(n, carry):
        cols = pl.ds(pl.multiple_of(n * chunk, chunk), chunk)
        both = dot(grads_t[...], rows[:, cols])
        gate_out[:, cols] = both[:ffw].astype(BF16)
        up_out[:, cols] = both[ffw:].astype(BF16)
        return carry

    lax.fori_loop(0, width // chunk, product, 0)


def outer_kernel(zn, ng, sc, *refs):
    hs, ds = refs[:zn], refs[zn : 2 * zn]
    own, sent, hidden, rows, sem = refs[2 * zn :]
    quad = hs[0].shape[0]
    copies = []
    for j in range(zn):
        copies.append(pltpu.make_async_copy(hs[j], hidden.at[pl.ds(j * quad, quad)], sem.at[2 * j]))
        copies.append(pltpu.make_async_copy(ds[j], rows.at[pl.ds(j * quad, quad)], sem.at[2 * j + 1]))
    for copy in copies:
        copy.start()
    for copy in copies:
        copy.wait()
    g = sc[3]
    width = own.shape[1]
    chunk = min(256, width)
    hidden_t = hidden[...].T

    for r in range(ng):
        base = lax.rem(g + r, ng) * width

        def product(n, carry):
            cols = pl.ds(pl.multiple_of(base + n * chunk, chunk), chunk)
            value = dot(hidden_t, rows[:, cols])
            to = pl.ds(pl.multiple_of(n * chunk, chunk), chunk)
            if r == 0:
                own[:, to] = value
            else:
                sent[r - 1, :, to] = value.astype(BF16)
            return carry

        lax.fori_loop(0, width // chunk, product, 0)


def per_device(
    tokens, d_out, expert_ids, gate_values, saved_gate_pre, saved_up_pre, w_gate, w_up, w_down
):
    tok, width = tokens.shape
    top = expert_ids.shape[1]
    ffw = saved_gate_pre.shape[2]
    nb, ng = lax.axis_size("blk"), lax.axis_size("grp")
    zn = nb // 4
    experts = w_gate.shape[0] * nb
    slots = 13 * tok // (2 * experts)
    block = -(-(slots + 1) // 8) * 8
    quad = 4 * block
    part = width // ng
    me, g = lax.axis_index("blk"), lax.axis_index("grp")
    z, x, c = me // 4, (me // 2) % 2, me % 2
    sc = jnp.stack([z, x, c, g]).astype(jnp.int32)

    def over_z(value, n):
        return lax.ppermute(value, "blk", [(b, b ^ (4 * n)) for b in range(nb)])

    def along_z(value, pairs):
        return lax.ppermute(value, "blk", [(4 * a + n, 4 * b + n) for a, b in pairs for n in range(4)])

    def over_x(value):
        return lax.ppermute(value, "blk", [(b, b ^ 2) for b in range(nb)])

    def over_core(value):
        return lax.ppermute(value, "blk", [(b, b ^ 1) for b in range(nb)])

    def over_groups(value, n):
        return lax.ppermute(value, "grp", [(b, (b + n) % ng) for b in range(ng)])

    def after(value, *others):
        return lax.optimization_barrier((value,) + others)[0]

    inner_plane = (z == 1) | (z == 2)
    middle, outward = [(1, 2), (2, 1)], [(1, 0), (2, 3)]
    smem = pl.BlockSpec(memory_space=pltpu.SMEM)
    vmem = pl.BlockSpec(memory_space=pltpu.VMEM)
    anywhere = pl.BlockSpec(memory_space=pl.ANY)

    def shape(*dims, dtype=BF16):
        return jax.ShapeDtypeStruct(dims, dtype)

    meta = jnp.concatenate([expert_ids.T.astype(BF16), gate_values.T], axis=0)
    def together(*values):
        return lax.optimization_barrier(values)

    keep, swap = pl.pallas_call(
        functools.partial(pack_kernel, top, slots, block),
        out_shape=[shape(zn, 2, block, 2 * ffw)] * 2,
        in_specs=[smem, vmem, anywhere, anywhere],
        out_specs=[vmem] * 2,
        scratch_shapes=[
            pltpu.VMEM((2 * ffw, top * tok), BF16),
            pltpu.SemaphoreType.DMA((2 * top,)),
        ],
        compiler_params=params(PACK),
        cost_estimate=cost(4 * experts * block * top * tok * ffw, 4 * top * tok * ffw),
        name="pack",
    )(sc, meta, saved_gate_pre.transpose(1, 2, 0), saved_up_pre.transpose(1, 2, 0))
    other = over_core(swap)
    pairs = [jnp.concatenate([keep[j], other[j]], axis=1) for j in range(zn)]

    mixed = [lax.dynamic_slice(tokens, (0, g * part), (tok, part))]
    for r in range(1, ng):
        there = lax.dynamic_slice(tokens, (0, ((g + r) % ng) * part), (tok, part))
        mixed.append(over_groups(there, r))
    mixed = jnp.concatenate(mixed, axis=0)
    weights = (w_gate[0].T, w_up[0].T, w_down[0])

    def expert(table, near, far):
        return pl.pallas_call(
            functools.partial(expert_kernel, slots, block),
            out_shape=[
                shape(quad, 2 * ffw),
                shape(quad, ffw),
                shape(quad, width),
                shape(block, width),
                shape(block, width),
                shape(2 * block, width),
            ],
            in_specs=[vmem] * 6 + [anywhere] * 3,
            out_specs=[vmem] * 6,
            scratch_shapes=[
                pltpu.VMEM((2 * ffw, width), BF16),
                pltpu.VMEM((2 * ffw, width), BF16),
                pltpu.SemaphoreType.DMA((4,)),
            ],
            compiler_params=params(EXPERT),
            cost_estimate=cost(2 * quad * width * (ffw * 4 + 4 * tok), 16e6),
            name="expert",
        )(*table, near, far, *weights)

    def combine(keep, swap, hop):
        return pl.pallas_call(
            functools.partial(combine_kernel, slots, block),
            out_shape=shape(tok, width),
            in_specs=[vmem] * 4,
            out_specs=vmem,
            compiler_params=params(COMBINE),
            cost_estimate=cost(2 * tok * 6 * block * width, 3e6),
            name="combine",
        )(keep, over_core(swap), hop, over_core(hop))

    def to_groups(value):
        return [value] + [over_groups(value, r) for r in range(1, ng)]

    def four(value, hop):
        return [value, over_core(value), hop, over_core(hop)]

    if zn == 4:
        d1, da, h0 = over_z(d_out, 1), along_z(d_out, middle), over_x(d_out)
        d1, da, h0, mixed, *pairs = together(d1, da, h0, mixed, *pairs)

        q1, db, h1 = over_z(pairs[1], 1), along_z(d1, middle), over_x(d1)
        c0, c1 = four(d_out, h0), over_core(d1)
        done = [expert(c0, pairs[0][0], over_x(pairs[0][1]))]
        q1, db, h1, c1, p2, da, *done[0] = together(q1, db, h1, c1, pairs[2], da, *done[0])

        q2, dc, f1 = over_z(p2, 2), along_z(da, outward), over_x(q1[1])
        back, grads = [over_x(done[0][5])], [to_groups(done[0][0])]
        mixed_hop = over_x(after(mixed, f1))
        done.append(expert([d1, c1, h1, over_core(h1)], q1[0], f1))
        q2, dc, mixed_hop, back[0], db, p3, *rest = together(
            q2, dc, mixed_hop, back[0], db, pairs[3], *grads[0], *done[1]
        )
        grads[0], done[1] = rest[:ng], rest[ng:]

        q3, dd, f2 = over_z(p3, 3), along_z(db, outward), over_x(q2[1])
        d2 = jnp.where(inner_plane, db, dc)
        h2 = over_x(d2)
        back.append(over_x(after(done[1][5], f2)))
        grads.append(to_groups(done[1][0]))
        sums = [combine(done[0][3], done[0][4], back[0])]
        done.append(expert(four(d2, h2), q2[0], f2))
        q3, dd, back[1], mixed, *rest = together(q3, dd, back[1], mixed, *grads[1], *done[2])
        grads[1], done[2] = rest[:ng], rest[ng:]

        m1, ma, f3 = over_z(mixed, 1), along_z(mixed, middle), over_x(q3[1])
        d3 = jnp.where(inner_plane, da, dd)
        h3 = over_x(d3)
        back.append(over_x(after(done[2][5], f3)))
        grads.append(to_groups(done[2][0]))
        mb, mc = along_z(m1, middle), along_z(ma, outward)
        sums.append(combine(done[1][3], done[1][4], back[1]))
        done.append(expert(four(d3, h3), q3[0], f3))
        m1, ma, mb, mc, back[2], sums[1], *rest = together(
            m1, ma, mb, mc, back[2], sums[1], *grads[2], *done[3]
        )
        grads[2], done[3] = rest[:ng], rest[ng:]

        md, m1_hop = along_z(mb, outward), over_x(m1)
        back.append(over_x(done[3][5]))
        grads.append(to_groups(done[3][0]))
        sums.append(combine(done[2][3], done[2][4], back[2]))
        inputs = four(mixed, mixed_hop) + four(m1, m1_hop)
        m2 = jnp.where(inner_plane, mb, mc)
        md, back[3], m2, *rest = together(md, back[3], m2, *inputs, *grads[3])
        inputs, grads[3] = rest[:8], rest[8:]

        m3 = jnp.where(inner_plane, ma, md)
        inputs += four(m2, over_x(m2)) + four(m3, over_x(m3))
        sums.append(combine(done[3][3], done[3][4], back[3]))
    else:
        done, grads, sums, inputs = [], [], [], []
        for j in range(zn):
            d, q, m = (over_z(v, j) if j else v for v in (d_out, pairs[j], mixed))
            done.append(expert(four(d, over_x(d)), q[0], over_x(q[1])))
            grads.append(to_groups(done[j][0]))
            sums.append(combine(done[j][3], done[j][4], over_x(done[j][5])))
            inputs += four(m, over_x(m))
    d_tokens = sums[0].astype(F32)
    for j in range(1, zn):
        d_tokens = d_tokens + over_z(sums[j], j).astype(F32)
    grads = [value for plane in grads for value in plane]

    down_own, down_sent = pl.pallas_call(
        functools.partial(outer_kernel, zn, ng),
        out_shape=[shape(ffw, part, dtype=F32), shape(max(ng - 1, 1), ffw, part)],
        in_specs=[smem] + [anywhere] * (2 * zn),
        out_specs=[vmem, vmem],
        scratch_shapes=[
            pltpu.VMEM((zn * quad, ffw), BF16),
            pltpu.VMEM((zn * quad, width), BF16),
            pltpu.SemaphoreType.DMA((2 * zn,)),
        ],
        compiler_params=params(OUTER),
        cost_estimate=cost(2 * zn * quad * ffw * width, 10e6),
        name="outer",
    )(sc, *[d[1] for d in done], *[d[2] for d in done])
    d_down = down_own
    for r in range(1, ng):
        d_down = d_down + over_groups(down_sent[r - 1], r).astype(F32)

    units = zn * ng
    d_gate, d_up = pl.pallas_call(
        functools.partial(inner_kernel, zn, ng, slots, block),
        out_shape=[shape(ffw, part)] * 2,
        in_specs=[anywhere] * (len(inputs) + len(grads)),
        out_specs=[vmem, vmem],
        scratch_shapes=[
            pltpu.VMEM((units, 4 * tok, part), BF16),
            pltpu.VMEM((units * quad, 2 * ffw), BF16),
            pltpu.VMEM((2 * ffw, units * quad), BF16),
            pltpu.VMEM((units * quad, part), BF16),
            pltpu.SemaphoreType.DMA((4 * units,)),
            pltpu.SemaphoreType.DMA((units,)),
        ],
        compiler_params=params(INNER if units <= 16 else 58),
        cost_estimate=cost(4 * units * quad * ffw * part, 20e6),
        name="inner",
    )(*inputs, *grads)
    return (
        d_tokens.astype(BF16),
        d_gate.T[None],
        d_up.T[None],
        d_down.astype(BF16)[None],
    )


def solution(mesh):
    return jax.shard_map(
        per_device,
        mesh=mesh,
        in_specs=(
            P(("grp", "blk"), None),
            P(("grp", "blk"), None),
            P(("grp", "blk"), None),
            P(("grp", "blk"), None),
            P(("grp", "blk"), None, None),
            P(("grp", "blk"), None, None),
            P("blk", None, None),
            P("blk", None, None),
            P("blk", None, None),
        ),
        out_specs=(
            P(("grp", "blk"), None),
            P("blk", "grp", None),
            P("blk", "grp", None),
            P("blk", None, "grp"),
        ),
        check_vma=False,
    )
```

```python
import functools

import jax
import jax.numpy as jnp
from jax import lax
from jax.experimental import pallas as pl
from jax.experimental.pallas import tpu as pltpu
from jax.sharding import PartitionSpec as P

BF16 = jnp.bfloat16
F32 = jnp.float32
MIB = 1024 * 1024
PACK, EXPERT, COMBINE, OUTER, INNER = 24, 40, 12, 24, 40
NT = (((1,), (1,)), ((), ()))
TN = (((0,), (0,)), ((), ()))


def params(mib):
    return pltpu.CompilerParams(vmem_limit_bytes=mib * MIB)


def cost(flops, moved):
    return pl.CostEstimate(flops=int(flops * 0.05), bytes_accessed=int(moved * 0.05), transcendentals=0)


def dot(a, b):
    return jnp.dot(a, b, preferred_element_type=F32)


def before_matrix(size):
    row = lax.broadcasted_iota(jnp.int32, (size, size), 0)
    col = lax.broadcasted_iota(jnp.int32, (size, size), 1)
    return jnp.where(row < col, 1.0, 0.0).astype(BF16)


def slot_rows(slot, count):
    row = lax.broadcasted_iota(jnp.int32, (count, slot.shape[1]), 0).astype(F32)
    return jnp.where(row == slot, 1.0, 0.0)


def moved(slot, by):
    return jnp.where(slot < 0, -1.0, slot + by)


def with_notes(rows, notes, slots, block):
    count, lanes = rows.shape[0], notes[0].shape[1]
    row = lax.rem(lax.broadcasted_iota(jnp.int32, (count, lanes), 0), block)
    spread = jnp.concatenate([jnp.broadcast_to(note, (block, lanes)) for note in notes], axis=0)
    return jnp.concatenate([jnp.where(row >= slots, spread, rows[:, :lanes]), rows[:, lanes:]], axis=1)


def pack_kernel(top, slots, block, sc, meta_ref, gate_pre, up_pre, keep, swap, cat, sem):
    ffw, tok = gate_pre.shape[1:]
    copies = []
    for part, src in enumerate((gate_pre, up_pre)):
        for k in range(top):
            copies.append(
                pltpu.make_async_copy(
                    src.at[k],
                    cat.at[pl.ds(part * ffw, ffw), pl.ds(k * tok, tok)],
                    sem.at[len(copies)],
                )
            )
    for copy in copies:
        copy.start()
    zn = keep.shape[0]
    experts = 4 * zn
    meta = meta_ref[...].astype(F32)
    order = lax.broadcasted_iota(jnp.int32, (experts, 1), 0)

    def turned(value, by):
        return lax.bitwise_xor(value, jnp.broadcast_to(by, value.shape))

    here = sc[0] * 4 + sc[1] * 2 + sc[2]
    across = jnp.where(order >= 2 * zn, 1, 0)
    expert = turned(lax.bitwise_and(order, 2 * zn - 1) * 2 + across, here).astype(F32)
    hits = [jnp.where(meta[k : k + 1] == expert, 1.0, 0.0) for k in range(top)]
    mask = sum(hits)
    slot = dot(mask.astype(BF16), before_matrix(tok))
    gates = sum(hits[k] * meta[top + k : top + k + 1] for k in range(top))
    notes = jnp.concatenate([jnp.where(mask > 0, slot, -1.0), gates], axis=1)
    place = slot + order.astype(F32) * block + 1.0
    target = jnp.concatenate(
        [jnp.sum(hits[k] * place, axis=0, keepdims=True) - 1.0 for k in range(top)], axis=1
    )
    for copy in copies:
        copy.wait()
    table = cat[...]
    lot = 4
    for first in range(0, experts, lot):
        pick = slot_rows(moved(target, -float(first * block)), lot * block).astype(BF16)
        packed = lax.dot_general(pick, table, NT, preferred_element_type=F32)
        packed = with_notes(packed, [notes[first + n : first + n + 1] for n in range(lot)], slots, block)
        for n in range(lot):
            at = (first + n) % (2 * zn)
            out = keep if first + n < 2 * zn else swap
            out[at // 2, at % 2] = packed[n * block : (n + 1) * block].astype(BF16)


def expert_kernel(
    slots, block, d00, d01, d10, d11, near, far, w_gate, w_up, w_down,
    grads_out, hidden_out, rows_out, keep_out, swap_out, hop_out, down_at, both_at, sem,
):
    ffw = w_down.shape[0]
    copies = [
        pltpu.make_async_copy(w_down, down_at.at[pl.ds(0, ffw)], sem.at[0]),
        pltpu.make_async_copy(w_down, down_at.at[pl.ds(ffw, ffw)], sem.at[1]),
        pltpu.make_async_copy(w_gate, both_at.at[pl.ds(0, ffw)], sem.at[2]),
        pltpu.make_async_copy(w_up, both_at.at[pl.ds(ffw, ffw)], sem.at[3]),
    ]
    for copy in copies:
        copy.start()
    tok = d00.shape[0]
    quad = 4 * block
    pre = jnp.concatenate([near[...].astype(F32), far[...].astype(F32)], axis=0)
    notes = [pre[n * block + slots : n * block + slots + 1, : 2 * tok] for n in range(4)]
    target = jnp.concatenate([moved(note[:, :tok], float(n * block)) for n, note in enumerate(notes)], axis=1)
    gates = jnp.concatenate([note[:, tok:] for note in notes], axis=1)
    pick = slot_rows(target, quad)
    weight = jnp.sum(pick * gates, axis=1, keepdims=True)
    table = jnp.concatenate([ref[...] for ref in (d00, d01, d10, d11)], axis=0)
    rows = dot(pick.astype(BF16), table).astype(BF16)
    rows_out[...] = rows
    copies[0].wait()
    copies[1].wait()
    back = lax.dot_general(rows, down_at[...], NT, preferred_element_type=F32)
    swapped = pltpu.roll(pre, ffw, axis=1)
    front = lax.broadcasted_iota(jnp.int32, pre.shape, 1) < ffw
    gate_pre = jnp.where(front, pre, swapped)
    up_pre = jnp.where(front, swapped, pre)
    sig = jax.nn.sigmoid(gate_pre)
    active = gate_pre * sig
    slope = jnp.where(front, up_pre * sig * (1.0 + gate_pre * (1.0 - sig)), active)
    grads = weight * back * slope
    hidden_out[...] = (weight * active * up_pre)[:, :ffw].astype(BF16)
    grads_out[...] = with_notes(grads, notes, slots, block).astype(BF16)
    copies[2].wait()
    copies[3].wait()
    route = with_notes(dot(grads.astype(BF16), both_at[...]), notes, slots, block).astype(BF16)
    keep_out[...] = route[:block]
    swap_out[...] = route[block : 2 * block]
    hop_out[...] = route[2 * block :]


def combine_kernel(slots, block, keep, swap, hop, hop_swap, out):
    tok = out.shape[0]
    total = jnp.zeros(out.shape, F32)
    for ref, start in ((keep, 0), (swap, 0), (hop, 0), (hop_swap, block)):
        rows = ref[...].astype(F32)
        slot = moved(rows[start + slots : start + slots + 1, :tok], float(start))
        pick = slot_rows(slot, rows.shape[0]).astype(BF16)
        total = total + lax.dot_general(pick, ref[...], TN, preferred_element_type=F32)
    out[...] = total.astype(BF16)


def inner_kernel(zn, ng, slots, block, *refs):
    n_x, n_g = 4 * zn, zn * ng
    xs, gs = refs[:n_x], refs[n_x : n_x + n_g]
    gate_out, up_out, table, grads, grads_t, rows, sem_x, sem_g = refs[n_x + n_g :]
    tok = xs[0].shape[0] // ng
    ffw, width = gate_out.shape
    quad = 4 * block
    units = n_g
    copies = []
    for u in range(units):
        j, r = u // ng, u % ng
        mine = [pltpu.make_async_copy(gs[u], grads.at[pl.ds(u * quad, quad)], sem_g.at[u])]
        for n in range(4):
            mine.append(
                pltpu.make_async_copy(
                    xs[4 * j + n].at[pl.ds(r * tok, tok)],
                    table.at[u, pl.ds(n * tok, tok)],
                    sem_x.at[4 * u + n],
                )
            )
        copies.append(mine)
        for copy in mine:
            copy.start()
    for u in range(units):
        for copy in copies[u]:
            copy.wait()
        targets = []
        for n in range(4):
            row = n * block + slots
            near = u * quad + row // 16 * 16
            note = grads[near : near + 16, :tok].astype(F32)[row % 16 : row % 16 + 1]
            targets.append(moved(note, float(n * block)))
        pick = slot_rows(jnp.concatenate(targets, axis=1), quad).astype(BF16)
        rows[u * quad : (u + 1) * quad, :] = dot(pick, table[u]).astype(BF16)
    total = units * quad
    step = 128
    for i in range(0, total, step):
        grads_t[:, i : i + step] = grads[i : i + step, :].T
    chunk = min(256, width)

    def product(n, carry):
        cols = pl.ds(pl.multiple_of(n * chunk, chunk), chunk)
        both = dot(grads_t[...], rows[:, cols])
        gate_out[:, cols] = both[:ffw].astype(BF16)
        up_out[:, cols] = both[ffw:].astype(BF16)
        return carry

    lax.fori_loop(0, width // chunk, product, 0)


def outer_kernel(zn, ng, sc, *refs):
    hs, ds = refs[:zn], refs[zn : 2 * zn]
    own, sent, hidden, rows, sem = refs[2 * zn :]
    quad = hs[0].shape[0]
    copies = []
    for j in range(zn):
        copies.append(pltpu.make_async_copy(hs[j], hidden.at[pl.ds(j * quad, quad)], sem.at[2 * j]))
        copies.append(pltpu.make_async_copy(ds[j], rows.at[pl.ds(j * quad, quad)], sem.at[2 * j + 1]))
    for copy in copies:
        copy.start()
    for copy in copies:
        copy.wait()
    g = sc[3]
    width = own.shape[1]
    chunk = min(256, width)
    hidden_t = hidden[...].T

    for r in range(ng):
        base = lax.rem(g + r, ng) * width

        def product(n, carry):
            cols = pl.ds(pl.multiple_of(base + n * chunk, chunk), chunk)
            value = dot(hidden_t, rows[:, cols])
            to = pl.ds(pl.multiple_of(n * chunk, chunk), chunk)
            if r == 0:
                own[:, to] = value
            else:
                sent[r - 1, :, to] = value.astype(BF16)
            return carry

        lax.fori_loop(0, width // chunk, product, 0)


def per_device(
    tokens, d_out, expert_ids, gate_values, saved_gate_pre, saved_up_pre, w_gate, w_up, w_down
):
    tok, width = tokens.shape
    top = expert_ids.shape[1]
    ffw = saved_gate_pre.shape[2]
    nb, ng = lax.axis_size("blk"), lax.axis_size("grp")
    zn = nb // 4
    experts = w_gate.shape[0] * nb
    slots = 13 * tok // (2 * experts)
    block = -(-(slots + 1) // 8) * 8
    quad = 4 * block
    part = width // ng
    me, g = lax.axis_index("blk"), lax.axis_index("grp")
    z, x, c = me // 4, (me // 2) % 2, me % 2
    sc = jnp.stack([z, x, c, g]).astype(jnp.int32)

    def over_z(value, n):
        return lax.ppermute(value, "blk", [(b, b ^ (4 * n)) for b in range(nb)])

    def along_z(value, pairs):
        return lax.ppermute(value, "blk", [(4 * a + n, 4 * b + n) for a, b in pairs for n in range(4)])

    def over_x(value):
        return lax.ppermute(value, "blk", [(b, b ^ 2) for b in range(nb)])

    def over_core(value):
        return lax.ppermute(value, "blk", [(b, b ^ 1) for b in range(nb)])

    def over_groups(value, n):
        return lax.ppermute(value, "grp", [(b, (b + n) % ng) for b in range(ng)])

    def after(value, *others):
        return lax.optimization_barrier((value,) + others)[0]

    inner_plane = (z == 1) | (z == 2)
    middle, outward = [(1, 2), (2, 1)], [(1, 0), (2, 3)]
    smem = pl.BlockSpec(memory_space=pltpu.SMEM)
    vmem = pl.BlockSpec(memory_space=pltpu.VMEM)
    anywhere = pl.BlockSpec(memory_space=pl.ANY)

    def shape(*dims, dtype=BF16):
        return jax.ShapeDtypeStruct(dims, dtype)

    meta = jnp.concatenate([expert_ids.T.astype(BF16), gate_values.T], axis=0)
    def together(*values):
        return lax.optimization_barrier(values)

    keep, swap = pl.pallas_call(
        functools.partial(pack_kernel, top, slots, block),
        out_shape=[shape(zn, 2, block, 2 * ffw)] * 2,
        in_specs=[smem, vmem, anywhere, anywhere],
        out_specs=[vmem] * 2,
        scratch_shapes=[
            pltpu.VMEM((2 * ffw, top * tok), BF16),
            pltpu.SemaphoreType.DMA((2 * top,)),
        ],
        compiler_params=params(PACK),
        cost_estimate=cost(4 * experts * block * top * tok * ffw, 4 * top * tok * ffw),
        name="pack",
    )(sc, meta, saved_gate_pre.transpose(1, 2, 0), saved_up_pre.transpose(1, 2, 0))
    other = over_core(swap)
    pairs = [jnp.concatenate([keep[j], other[j]], axis=1) for j in range(zn)]

    mixed = [lax.dynamic_slice(tokens, (0, g * part), (tok, part))]
    for r in range(1, ng):
        there = lax.dynamic_slice(tokens, (0, ((g + r) % ng) * part), (tok, part))
        mixed.append(over_groups(there, r))
    mixed = jnp.concatenate(mixed, axis=0)
    weights = (w_gate[0].T, w_up[0].T, w_down[0])

    def expert(table, near, far):
        return pl.pallas_call(
            functools.partial(expert_kernel, slots, block),
            out_shape=[
                shape(quad, 2 * ffw),
                shape(quad, ffw),
                shape(quad, width),
                shape(block, width),
                shape(block, width),
                shape(2 * block, width),
            ],
            in_specs=[vmem] * 6 + [anywhere] * 3,
            out_specs=[vmem] * 6,
            scratch_shapes=[
                pltpu.VMEM((2 * ffw, width), BF16),
                pltpu.VMEM((2 * ffw, width), BF16),
                pltpu.SemaphoreType.DMA((4,)),
            ],
            compiler_params=params(EXPERT),
            cost_estimate=cost(2 * quad * width * (ffw * 4 + 4 * tok), 16e6),
            name="expert",
        )(*table, near, far, *weights)

    def combine(keep, swap, hop):
        return pl.pallas_call(
            functools.partial(combine_kernel, slots, block),
            out_shape=shape(tok, width),
            in_specs=[vmem] * 4,
            out_specs=vmem,
            compiler_params=params(COMBINE),
            cost_estimate=cost(2 * tok * 6 * block * width, 3e6),
            name="combine",
        )(keep, over_core(swap), hop, over_core(hop))

    def to_groups(value):
        return [value] + [over_groups(value, r) for r in range(1, ng)]

    def four(value, hop):
        return [value, over_core(value), hop, over_core(hop)]

    if zn == 4:
        d1, da, h0 = over_z(d_out, 1), along_z(d_out, middle), over_x(d_out)
        d1, da, h0, mixed, *pairs = together(d1, da, h0, mixed, *pairs)

        q1, db, h1 = over_z(pairs[1], 1), along_z(d1, middle), over_x(d1)
        c0, c1 = four(d_out, h0), over_core(d1)
        done = [expert(c0, pairs[0][0], over_x(pairs[0][1]))]
        q1, db, h1, c1, p2, da, *done[0] = together(q1, db, h1, c1, pairs[2], da, *done[0])

        q2, dc, f1 = over_z(p2, 2), along_z(da, outward), over_x(q1[1])
        back, grads = [over_x(done[0][5])], [to_groups(done[0][0])]
        mixed_hop = over_x(after(mixed, f1))
        done.append(expert([d1, c1, h1, over_core(h1)], q1[0], f1))
        q2, dc, mixed_hop, back[0], db, p3, *rest = together(
            q2, dc, mixed_hop, back[0], db, pairs[3], *grads[0], *done[1]
        )
        grads[0], done[1] = rest[:ng], rest[ng:]

        q3, dd, f2 = over_z(p3, 3), along_z(db, outward), over_x(q2[1])
        d2 = jnp.where(inner_plane, db, dc)
        h2 = over_x(d2)
        back.append(over_x(after(done[1][5], f2)))
        grads.append(to_groups(done[1][0]))
        sums = [combine(done[0][3], done[0][4], back[0])]
        done.append(expert(four(d2, h2), q2[0], f2))
        q3, dd, back[1], mixed, *rest = together(q3, dd, back[1], mixed, *grads[1], *done[2])
        grads[1], done[2] = rest[:ng], rest[ng:]

        m1, ma, f3 = over_z(mixed, 1), along_z(mixed, middle), over_x(q3[1])
        d3 = jnp.where(inner_plane, da, dd)
        h3 = over_x(d3)
        back.append(over_x(after(done[2][5], f3)))
        grads.append(to_groups(done[2][0]))
        mb, mc = along_z(m1, middle), along_z(ma, outward)
        sums.append(combine(done[1][3], done[1][4], back[1]))
        done.append(expert(four(d3, h3), q3[0], f3))
        m1, ma, mb, mc, back[2], sums[1], *rest = together(
            m1, ma, mb, mc, back[2], sums[1], *grads[2], *done[3]
        )
        grads[2], done[3] = rest[:ng], rest[ng:]

        md, m1_hop = along_z(mb, outward), over_x(m1)
        back.append(over_x(done[3][5]))
        grads.append(to_groups(done[3][0]))
        sums.append(combine(done[2][3], done[2][4], back[2]))
        inputs = four(mixed, mixed_hop) + four(m1, m1_hop)
        m2 = jnp.where(inner_plane, mb, mc)
        md, back[3], m2, *rest = together(md, back[3], m2, *inputs, *grads[3])
        inputs, grads[3] = rest[:8], rest[8:]

        m3 = jnp.where(inner_plane, ma, md)
        inputs += four(m2, over_x(m2)) + four(m3, over_x(m3))
        sums.append(combine(done[3][3], done[3][4], back[3]))
    else:
        done, grads, sums, inputs = [], [], [], []
        for j in range(zn):
            d, q, m = (over_z(v, j) if j else v for v in (d_out, pairs[j], mixed))
            done.append(expert(four(d, over_x(d)), q[0], over_x(q[1])))
            grads.append(to_groups(done[j][0]))
            sums.append(combine(done[j][3], done[j][4], over_x(done[j][5])))
            inputs += four(m, over_x(m))
    d_tokens = sums[0].astype(F32)
    for j in range(1, zn):
        d_tokens = d_tokens + over_z(sums[j], j).astype(F32)
    grads = [value for plane in grads for value in plane]

    down_own, down_sent = pl.pallas_call(
        functools.partial(outer_kernel, zn, ng),
        out_shape=[shape(ffw, part, dtype=F32), shape(max(ng - 1, 1), ffw, part)],
        in_specs=[smem] + [anywhere] * (2 * zn),
        out_specs=[vmem, vmem],
        scratch_shapes=[
            pltpu.VMEM((zn * quad, ffw), BF16),
            pltpu.VMEM((zn * quad, width), BF16),
            pltpu.SemaphoreType.DMA((2 * zn,)),
        ],
        compiler_params=params(OUTER),
        cost_estimate=cost(2 * zn * quad * ffw * width, 10e6),
        name="outer",
    )(sc, *[d[1] for d in done], *[d[2] for d in done])
    d_down = down_own
    for r in range(1, ng):
        d_down = d_down + over_groups(down_sent[r - 1], r).astype(F32)

    units = zn * ng
    d_gate, d_up = pl.pallas_call(
        functools.partial(inner_kernel, zn, ng, slots, block),
        out_shape=[shape(ffw, part)] * 2,
        in_specs=[anywhere] * (len(inputs) + len(grads)),
        out_specs=[vmem, vmem],
        scratch_shapes=[
            pltpu.VMEM((units, 4 * tok, part), BF16),
            pltpu.VMEM((units * quad, 2 * ffw), BF16),
            pltpu.VMEM((2 * ffw, units * quad), BF16),
            pltpu.VMEM((units * quad, part), BF16),
            pltpu.SemaphoreType.DMA((4 * units,)),
            pltpu.SemaphoreType.DMA((units,)),
        ],
        compiler_params=params(INNER if units <= 16 else 58),
        cost_estimate=cost(4 * units * quad * ffw * part, 20e6),
        name="inner",
    )(*inputs, *grads)
    return (
        d_tokens.astype(BF16),
        d_gate.T[None],
        d_up.T[None],
        d_down.astype(BF16)[None],
    )


def solution(mesh):
    return jax.shard_map(
        per_device,
        mesh=mesh,
        in_specs=(
            P(("grp", "blk"), None),
            P(("grp", "blk"), None),
            P(("grp", "blk"), None),
            P(("grp", "blk"), None),
            P(("grp", "blk"), None, None),
            P(("grp", "blk"), None, None),
            P("blk", None, None),
            P("blk", None, None),
            P("blk", None, None),
        ),
        out_specs=(
            P(("grp", "blk"), None),
            P("blk", "grp", None),
            P("blk", "grp", None),
            P("blk", None, "grp"),
        ),
        check_vma=False,
    )
```

```python
import functools

import jax
import jax.numpy as jnp
from jax import lax
from jax.experimental import pallas as pl
from jax.experimental.pallas import tpu as pltpu
from jax.sharding import PartitionSpec as P

BF16 = jnp.bfloat16
F32 = jnp.float32
MIB = 1024 * 1024
PACK, EXPERT, COMBINE, OUTER, INNER = 20, 30, 8, 20, 36
NT = (((1,), (1,)), ((), ()))
TN = (((0,), (0,)), ((), ()))


def params(mib):
    return pltpu.CompilerParams(vmem_limit_bytes=mib * MIB)


def cost(flops, moved):
    return pl.CostEstimate(flops=int(flops * 0.05), bytes_accessed=int(moved * 0.05), transcendentals=0)


def dot(a, b):
    return jnp.dot(a, b, preferred_element_type=F32)


def before_matrix(size):
    row = lax.broadcasted_iota(jnp.int32, (size, size), 0)
    col = lax.broadcasted_iota(jnp.int32, (size, size), 1)
    return jnp.where(row < col, 1.0, 0.0).astype(BF16)


def slot_rows(slot, count):
    row = lax.broadcasted_iota(jnp.int32, (count, slot.shape[1]), 0).astype(F32)
    return jnp.where(row == slot, 1.0, 0.0)


def moved(slot, by):
    return jnp.where(slot < 0, -1.0, slot + by)


def with_notes(rows, notes, slots, block):
    count, lanes = rows.shape[0], notes[0].shape[1]
    row = lax.rem(lax.broadcasted_iota(jnp.int32, (count, lanes), 0), block)
    spread = jnp.concatenate([jnp.broadcast_to(note, (block, lanes)) for note in notes], axis=0)
    return jnp.concatenate([jnp.where(row >= slots, spread, rows[:, :lanes]), rows[:, lanes:]], axis=1)


def pack_kernel(top, slots, block, sc, meta_ref, gate_pre, up_pre, keep, swap, cat, sem):
    ffw, tok = gate_pre.shape[1:]
    copies = []
    for part, src in enumerate((gate_pre, up_pre)):
        for k in range(top):
            copies.append(
                pltpu.make_async_copy(
                    src.at[k],
                    cat.at[pl.ds(part * ffw, ffw), pl.ds(k * tok, tok)],
                    sem.at[len(copies)],
                )
            )
    for copy in copies:
        copy.start()
    zn = keep.shape[0]
    experts = 4 * zn
    meta = meta_ref[...].astype(F32)
    order = lax.broadcasted_iota(jnp.int32, (experts, 1), 0)

    def turned(value, by):
        return lax.bitwise_xor(value, jnp.broadcast_to(by, value.shape))

    here = sc[0] * 4 + sc[1] * 2 + sc[2]
    across = jnp.where(order >= 2 * zn, 1, 0)
    expert = turned(lax.bitwise_and(order, 2 * zn - 1) * 2 + across, here).astype(F32)
    hits = [jnp.where(meta[k : k + 1] == expert, 1.0, 0.0) for k in range(top)]
    mask = sum(hits)
    slot = dot(mask.astype(BF16), before_matrix(tok))
    gates = sum(hits[k] * meta[top + k : top + k + 1] for k in range(top))
    notes = jnp.concatenate([jnp.where(mask > 0, slot, -1.0), gates], axis=1)
    place = slot + order.astype(F32) * block + 1.0
    target = jnp.concatenate(
        [jnp.sum(hits[k] * place, axis=0, keepdims=True) - 1.0 for k in range(top)], axis=1
    )
    for copy in copies:
        copy.wait()
    table = cat[...]
    lot = 4
    for first in range(0, experts, lot):
        pick = slot_rows(moved(target, -float(first * block)), lot * block).astype(BF16)
        packed = lax.dot_general(pick, table, NT, preferred_element_type=F32)
        packed = with_notes(packed, [notes[first + n : first + n + 1] for n in range(lot)], slots, block)
        for n in range(lot):
            at = (first + n) % (2 * zn)
            out = keep if first + n < 2 * zn else swap
            out[at // 2, at % 2] = packed[n * block : (n + 1) * block].astype(BF16)


def expert_kernel(
    slots, block, d00, d01, d10, d11, near, far, w_gate, w_up, w_down,
    grads_out, hidden_out, rows_out, keep_out, swap_out, hop_out, down_at, both_at, sem,
):
    ffw = w_down.shape[0]
    copies = [
        pltpu.make_async_copy(w_down, down_at.at[pl.ds(0, ffw)], sem.at[0]),
        pltpu.make_async_copy(w_down, down_at.at[pl.ds(ffw, ffw)], sem.at[1]),
        pltpu.make_async_copy(w_gate, both_at.at[pl.ds(0, ffw)], sem.at[2]),
        pltpu.make_async_copy(w_up, both_at.at[pl.ds(ffw, ffw)], sem.at[3]),
    ]
    for copy in copies:
        copy.start()
    tok = d00.shape[0]
    quad = 4 * block
    pre = jnp.concatenate([near[...].astype(F32), far[...].astype(F32)], axis=0)
    notes = [pre[n * block + slots : n * block + slots + 1, : 2 * tok] for n in range(4)]
    target = jnp.concatenate([moved(note[:, :tok], float(n * block)) for n, note in enumerate(notes)], axis=1)
    gates = jnp.concatenate([note[:, tok:] for note in notes], axis=1)
    pick = slot_rows(target, quad)
    weight = jnp.sum(pick * gates, axis=1, keepdims=True)
    table = jnp.concatenate([ref[...] for ref in (d00, d01, d10, d11)], axis=0)
    rows = dot(pick.astype(BF16), table).astype(BF16)
    rows_out[...] = rows
    copies[0].wait()
    copies[1].wait()
    back = lax.dot_general(rows, down_at[...], NT, preferred_element_type=F32)
    swapped = pltpu.roll(pre, ffw, axis=1)
    front = lax.broadcasted_iota(jnp.int32, pre.shape, 1) < ffw
    gate_pre = jnp.where(front, pre, swapped)
    up_pre = jnp.where(front, swapped, pre)
    sig = jax.nn.sigmoid(gate_pre)
    active = gate_pre * sig
    slope = jnp.where(front, up_pre * sig * (1.0 + gate_pre * (1.0 - sig)), active)
    grads = weight * back * slope
    hidden_out[...] = (weight * active * up_pre)[:, :ffw].astype(BF16)
    grads_out[...] = with_notes(grads, notes, slots, block).astype(BF16)
    copies[2].wait()
    copies[3].wait()
    route = with_notes(dot(grads.astype(BF16), both_at[...]), notes, slots, block).astype(BF16)
    keep_out[...] = route[:block]
    swap_out[...] = route[block : 2 * block]
    hop_out[...] = route[2 * block :]


def combine_kernel(slots, block, keep, swap, hop, hop_swap, out):
    tok = out.shape[0]
    total = jnp.zeros(out.shape, F32)
    for ref, start in ((keep, 0), (swap, 0), (hop, 0), (hop_swap, block)):
        rows = ref[...].astype(F32)
        slot = moved(rows[start + slots : start + slots + 1, :tok], float(start))
        pick = slot_rows(slot, rows.shape[0]).astype(BF16)
        total = total + lax.dot_general(pick, ref[...], TN, preferred_element_type=F32)
    out[...] = total.astype(BF16)


def inner_kernel(zn, ng, slots, block, *refs):
    n_x, n_g = 4 * zn, zn * ng
    xs, gs = refs[:n_x], refs[n_x : n_x + n_g]
    gate_out, up_out, table, grads, grads_t, rows, sem_x, sem_g = refs[n_x + n_g :]
    tok = xs[0].shape[0] // ng
    ffw, width = gate_out.shape
    quad = 4 * block
    units = n_g
    copies = []
    for u in range(units):
        j, r = u // ng, u % ng
        mine = [pltpu.make_async_copy(gs[u], grads.at[pl.ds(u * quad, quad)], sem_g.at[u])]
        for n in range(4):
            mine.append(
                pltpu.make_async_copy(
                    xs[4 * j + n].at[pl.ds(r * tok, tok)],
                    table.at[u, pl.ds(n * tok, tok)],
                    sem_x.at[4 * u + n],
                )
            )
        copies.append(mine)
        for copy in mine:
            copy.start()
    for u in range(units):
        for copy in copies[u]:
            copy.wait()
        targets = []
        for n in range(4):
            row = n * block + slots
            near = u * quad + row // 16 * 16
            note = grads[near : near + 16, :tok].astype(F32)[row % 16 : row % 16 + 1]
            targets.append(moved(note, float(n * block)))
        pick = slot_rows(jnp.concatenate(targets, axis=1), quad).astype(BF16)
        rows[u * quad : (u + 1) * quad, :] = dot(pick, table[u]).astype(BF16)
    total = units * quad
    step = 128
    for i in range(0, total, step):
        grads_t[:, i : i + step] = grads[i : i + step, :].T
    chunk = min(256, width)

    def product(n, carry):
        cols = pl.ds(pl.multiple_of(n * chunk, chunk), chunk)
        both = dot(grads_t[...], rows[:, cols])
        gate_out[:, cols] = both[:ffw].astype(BF16)
        up_out[:, cols] = both[ffw:].astype(BF16)
        return carry

    lax.fori_loop(0, width // chunk, product, 0)


def outer_kernel(zn, ng, sc, *refs):
    hs, ds = refs[:zn], refs[zn : 2 * zn]
    own, sent, hidden, rows, sem = refs[2 * zn :]
    quad = hs[0].shape[0]
    copies = []
    for j in range(zn):
        copies.append(pltpu.make_async_copy(hs[j], hidden.at[pl.ds(j * quad, quad)], sem.at[2 * j]))
        copies.append(pltpu.make_async_copy(ds[j], rows.at[pl.ds(j * quad, quad)], sem.at[2 * j + 1]))
    for copy in copies:
        copy.start()
    for copy in copies:
        copy.wait()
    g = sc[3]
    width = own.shape[1]
    chunk = min(256, width)
    hidden_t = hidden[...].T

    for r in range(ng):
        base = lax.rem(g + r, ng) * width

        def product(n, carry):
            cols = pl.ds(pl.multiple_of(base + n * chunk, chunk), chunk)
            value = dot(hidden_t, rows[:, cols])
            to = pl.ds(pl.multiple_of(n * chunk, chunk), chunk)
            if r == 0:
                own[:, to] = value
            else:
                sent[r - 1, :, to] = value.astype(BF16)
            return carry

        lax.fori_loop(0, width // chunk, product, 0)


def per_device(
    tokens, d_out, expert_ids, gate_values, saved_gate_pre, saved_up_pre, w_gate, w_up, w_down
):
    tok, width = tokens.shape
    top = expert_ids.shape[1]
    ffw = saved_gate_pre.shape[2]
    nb, ng = lax.axis_size("blk"), lax.axis_size("grp")
    zn = nb // 4
    experts = w_gate.shape[0] * nb
    slots = 13 * tok // (2 * experts)
    block = -(-(slots + 1) // 8) * 8
    quad = 4 * block
    part = width // ng
    me, g = lax.axis_index("blk"), lax.axis_index("grp")
    z, x, c = me // 4, (me // 2) % 2, me % 2
    sc = jnp.stack([z, x, c, g]).astype(jnp.int32)

    def over_z(value, n):
        return lax.ppermute(value, "blk", [(b, b ^ (4 * n)) for b in range(nb)])

    def along_z(value, pairs):
        return lax.ppermute(value, "blk", [(4 * a + n, 4 * b + n) for a, b in pairs for n in range(4)])

    def over_x(value):
        return lax.ppermute(value, "blk", [(b, b ^ 2) for b in range(nb)])

    def over_core(value):
        return lax.ppermute(value, "blk", [(b, b ^ 1) for b in range(nb)])

    def over_groups(value, n):
        return lax.ppermute(value, "grp", [(b, (b + n) % ng) for b in range(ng)])

    def after(value, *others):
        return lax.optimization_barrier((value,) + others)[0]

    inner_plane = (z == 1) | (z == 2)
    middle, outward = [(1, 2), (2, 1)], [(1, 0), (2, 3)]
    smem = pl.BlockSpec(memory_space=pltpu.SMEM)
    vmem = pl.BlockSpec(memory_space=pltpu.VMEM)
    anywhere = pl.BlockSpec(memory_space=pl.ANY)

    def shape(*dims, dtype=BF16):
        return jax.ShapeDtypeStruct(dims, dtype)

    meta = jnp.concatenate([expert_ids.T.astype(BF16), gate_values.T], axis=0)
    def together(*values):
        return lax.optimization_barrier(values)

    keep, swap = pl.pallas_call(
        functools.partial(pack_kernel, top, slots, block),
        out_shape=[shape(zn, 2, block, 2 * ffw)] * 2,
        in_specs=[smem, vmem, anywhere, anywhere],
        out_specs=[vmem] * 2,
        scratch_shapes=[
            pltpu.VMEM((2 * ffw, top * tok), BF16),
            pltpu.SemaphoreType.DMA((2 * top,)),
        ],
        compiler_params=params(PACK),
        cost_estimate=cost(4 * experts * block * top * tok * ffw, 4 * top * tok * ffw),
        name="pack",
    )(sc, meta, saved_gate_pre.transpose(1, 2, 0), saved_up_pre.transpose(1, 2, 0))
    other = over_core(swap)
    pairs = [jnp.concatenate([keep[j], other[j]], axis=1) for j in range(zn)]

    mixed = [lax.dynamic_slice(tokens, (0, g * part), (tok, part))]
    for r in range(1, ng):
        there = lax.dynamic_slice(tokens, (0, ((g + r) % ng) * part), (tok, part))
        mixed.append(over_groups(there, r))
    mixed = jnp.concatenate(mixed, axis=0)
    weights = (w_gate[0].T, w_up[0].T, w_down[0])

    def expert(table, near, far):
        return pl.pallas_call(
            functools.partial(expert_kernel, slots, block),
            out_shape=[
                shape(quad, 2 * ffw),
                shape(quad, ffw),
                shape(quad, width),
                shape(block, width),
                shape(block, width),
                shape(2 * block, width),
            ],
            in_specs=[vmem] * 6 + [anywhere] * 3,
            out_specs=[vmem] * 6,
            scratch_shapes=[
                pltpu.VMEM((2 * ffw, width), BF16),
                pltpu.VMEM((2 * ffw, width), BF16),
                pltpu.SemaphoreType.DMA((4,)),
            ],
            compiler_params=params(EXPERT),
            cost_estimate=cost(2 * quad * width * (ffw * 4 + 4 * tok), 16e6),
            name="expert",
        )(*table, near, far, *weights)

    def combine(keep, swap, hop):
        return pl.pallas_call(
            functools.partial(combine_kernel, slots, block),
            out_shape=shape(tok, width),
            in_specs=[vmem] * 4,
            out_specs=vmem,
            compiler_params=params(COMBINE),
            cost_estimate=cost(2 * tok * 6 * block * width, 3e6),
            name="combine",
        )(keep, over_core(swap), hop, over_core(hop))

    def to_groups(value):
        return [value] + [over_groups(value, r) for r in range(1, ng)]

    def four(value, hop):
        return [value, over_core(value), hop, over_core(hop)]

    if zn == 4:
        d1, da, h0 = over_z(d_out, 1), along_z(d_out, middle), over_x(d_out)
        d1, da, h0, mixed, *pairs = together(d1, da, h0, mixed, *pairs)

        q1, db, h1 = over_z(pairs[1], 1), along_z(d1, middle), over_x(d1)
        c0, c1 = four(d_out, h0), over_core(d1)
        done = [expert(c0, pairs[0][0], over_x(pairs[0][1]))]
        q1, db, h1, c1, p2, da, *done[0] = together(q1, db, h1, c1, pairs[2], da, *done[0])

        q2, dc, f1 = over_z(p2, 2), along_z(da, outward), over_x(q1[1])
        back, grads = [over_x(done[0][5])], [to_groups(done[0][0])]
        mixed_hop = over_x(after(mixed, f1))
        done.append(expert([d1, c1, h1, over_core(h1)], q1[0], f1))
        q2, dc, mixed_hop, back[0], db, p3, *rest = together(
            q2, dc, mixed_hop, back[0], db, pairs[3], *grads[0], *done[1]
        )
        grads[0], done[1] = rest[:ng], rest[ng:]

        q3, dd, f2 = over_z(p3, 3), along_z(db, outward), over_x(q2[1])
        d2 = jnp.where(inner_plane, db, dc)
        h2 = over_x(d2)
        back.append(over_x(after(done[1][5], f2)))
        grads.append(to_groups(done[1][0]))
        sums = [combine(done[0][3], done[0][4], back[0])]
        done.append(expert(four(d2, h2), q2[0], f2))
        q3, dd, back[1], mixed, *rest = together(q3, dd, back[1], mixed, *grads[1], *done[2])
        grads[1], done[2] = rest[:ng], rest[ng:]

        m1, ma, f3 = over_z(mixed, 1), along_z(mixed, middle), over_x(q3[1])
        d3 = jnp.where(inner_plane, da, dd)
        h3 = over_x(d3)
        back.append(over_x(after(done[2][5], f3)))
        grads.append(to_groups(done[2][0]))
        mb, mc = along_z(m1, middle), along_z(ma, outward)
        sums.append(combine(done[1][3], done[1][4], back[1]))
        done.append(expert(four(d3, h3), q3[0], f3))
        m1, ma, mb, mc, back[2], sums[1], *rest = together(
            m1, ma, mb, mc, back[2], sums[1], *grads[2], *done[3]
        )
        grads[2], done[3] = rest[:ng], rest[ng:]

        md, m1_hop = along_z(mb, outward), over_x(m1)
        back.append(over_x(done[3][5]))
        grads.append(to_groups(done[3][0]))
        sums.append(combine(done[2][3], done[2][4], back[2]))
        inputs = four(mixed, mixed_hop) + four(m1, m1_hop)
        m2 = jnp.where(inner_plane, mb, mc)
        md, back[3], m2, *rest = together(md, back[3], m2, *inputs, *grads[3])
        inputs, grads[3] = rest[:8], rest[8:]

        m3 = jnp.where(inner_plane, ma, md)
        inputs += four(m2, over_x(m2)) + four(m3, over_x(m3))
        sums.append(combine(done[3][3], done[3][4], back[3]))
    else:
        done, grads, sums, inputs = [], [], [], []
        for j in range(zn):
            d, q, m = (over_z(v, j) if j else v for v in (d_out, pairs[j], mixed))
            done.append(expert(four(d, over_x(d)), q[0], over_x(q[1])))
            grads.append(to_groups(done[j][0]))
            sums.append(combine(done[j][3], done[j][4], over_x(done[j][5])))
            inputs += four(m, over_x(m))
    d_tokens = sums[0].astype(F32)
    for j in range(1, zn):
        d_tokens = d_tokens + over_z(sums[j], j).astype(F32)
    grads = [value for plane in grads for value in plane]

    down_own, down_sent = pl.pallas_call(
        functools.partial(outer_kernel, zn, ng),
        out_shape=[shape(ffw, part, dtype=F32), shape(max(ng - 1, 1), ffw, part)],
        in_specs=[smem] + [anywhere] * (2 * zn),
        out_specs=[vmem, vmem],
        scratch_shapes=[
            pltpu.VMEM((zn * quad, ffw), BF16),
            pltpu.VMEM((zn * quad, width), BF16),
            pltpu.SemaphoreType.DMA((2 * zn,)),
        ],
        compiler_params=params(OUTER),
        cost_estimate=cost(2 * zn * quad * ffw * width, 10e6),
        name="outer",
    )(sc, *[d[1] for d in done], *[d[2] for d in done])
    d_down = down_own
    for r in range(1, ng):
        d_down = d_down + over_groups(down_sent[r - 1], r).astype(F32)

    units = zn * ng
    d_gate, d_up = pl.pallas_call(
        functools.partial(inner_kernel, zn, ng, slots, block),
        out_shape=[shape(ffw, part)] * 2,
        in_specs=[anywhere] * (len(inputs) + len(grads)),
        out_specs=[vmem, vmem],
        scratch_shapes=[
            pltpu.VMEM((units, 4 * tok, part), BF16),
            pltpu.VMEM((units * quad, 2 * ffw), BF16),
            pltpu.VMEM((2 * ffw, units * quad), BF16),
            pltpu.VMEM((units * quad, part), BF16),
            pltpu.SemaphoreType.DMA((4 * units,)),
            pltpu.SemaphoreType.DMA((units,)),
        ],
        compiler_params=params(INNER if units <= 16 else 58),
        cost_estimate=cost(4 * units * quad * ffw * part, 20e6),
        name="inner",
    )(*inputs, *grads)
    return (
        d_tokens.astype(BF16),
        d_gate.T[None],
        d_up.T[None],
        d_down.astype(BF16)[None],
    )


def solution(mesh):
    return jax.shard_map(
        per_device,
        mesh=mesh,
        in_specs=(
            P(("grp", "blk"), None),
            P(("grp", "blk"), None),
            P(("grp", "blk"), None),
            P(("grp", "blk"), None),
            P(("grp", "blk"), None, None),
            P(("grp", "blk"), None, None),
            P("blk", None, None),
            P("blk", None, None),
            P("blk", None, None),
        ),
        out_specs=(
            P(("grp", "blk"), None),
            P("blk", "grp", None),
            P("blk", "grp", None),
            P("blk", None, "grp"),
        ),
        check_vma=False,
    )
```
